32 devices in a mesh: groups: 2 (over x), expert: 16 (over z, y, core).
Axes of the slice: x: 2, y: 2, z: 4, core: 2. Of those that a mesh axis runs over, the one named last changes fastest.
Arguments:
- tokens: bfloat16 [2048, 2048], P(('groups', 'expert')), parts along dimension 0, may hold values from -6 to 6
- out_grad: bfloat16 [2048, 2048], P(('groups', 'expert')), parts along dimension 0, may hold values from -6 to 6
- routes: int32 [2048, 8], P(('groups', 'expert')), parts along dimension 0, may hold values from 0 to 15, all different within a row; in each aligned block of 64 rows (0 to 63, 64 to 127, ...) at most 40 rows name the same one
- route_weights: bfloat16 [2048, 8], P(('groups', 'expert')), parts along dimension 0, may hold values from 0.049804688 to 0.29882812
- gate_weight: bfloat16 [16, 2048, 768], P('expert'), may hold values from -0.125 to 0.125
- up_weight: bfloat16 [16, 2048, 768], P('expert'), may hold values from -0.125 to 0.125
- down_weight: bfloat16 [16, 768, 2048], P('expert'), may hold values from -0.21875 to 0.21875
- gate_adapter_input: bfloat16 [16, 16, 2048], P('expert'), may hold values from -0.125 to 0.125
- gate_adapter_output: bfloat16 [16, 16, 768], P('expert'), may hold values from -1.5 to 1.5
- up_adapter_input: bfloat16 [16, 16, 2048], P('expert'), may hold values from -0.125 to 0.125
- up_adapter_output: bfloat16 [16, 16, 768], P('expert'), may hold values from -1.5 to 1.5
- down_adapter_input: bfloat16 [16, 16, 768], P('expert'), may hold values from -0.21875 to 0.21875
- down_adapter_output: bfloat16 [16, 16, 2048], P('expert'), may hold values from -1.5 to 1.5
Outputs:
- grad_tokens: bfloat16 [2048, 2048], P(('groups', 'expert')), parts along dimension 0
- grad_weights: float32 [2048, 8], P(('groups', 'expert')), parts along dimension 0
- grad_a_gate: float32 [32, 16, 2048], P(('groups', 'expert')), parts along dimension 0
- grad_b_gate: float32 [32, 16, 768], P(('groups', 'expert')), parts along dimension 0
- grad_a_up: float32 [32, 16, 2048], P(('groups', 'expert')), parts along dimension 0
- grad_b_up: float32 [32, 16, 768], P(('groups', 'expert')), parts along dimension 0
- grad_a_down: float32 [32, 16, 768], P(('groups', 'expert')), parts along dimension 0
- grad_b_down: float32 [32, 16, 2048], P(('groups', 'expert')), parts along dimension 0
The draws below stay inside these ranges and needn't reach their ends.
There are 2 independent parts, one for each index of `groups`. The reference program is written for one: setup_inputs(seed, part) draws one part's arguments, and reference() takes and returns one part's arrays. A program takes and returns all parts, laid end to end along the dimension named above; an argument that names none is the same for every part. Nothing has to cross between parts.
Inputs may be any that keep to these rules, and one draw needn't show every extreme that they name: `routes`: each row names 8 different experts, and every expert is named by some row. Among the rows of one index of expert (aligned blocks of 64 rows), no expert is named more than 40 times, a bound that some block reaches.
All inputs are finite; a program needn't handle non-finite values.
Results may differ from the reference program's by a relative error of at most 0.0068.
Values may be sent and summed in bfloat16 or wider, within the bound.
A program may use at most 128 MiB of HBM per device.

```python
import math
import jax
import jax.numpy as jnp
import numpy as np
from jax import lax

D = 2048
H = 768
R = 16
TOP = 8
TOK_DEV = 64
EXPERTS = 16
TOKENS = 1024
CAP = 40
N_EXPERT = 16


def level_of(key, shape, cuts, smallest, top_value):
    level, own = 1.0, jax.random.fold_in(key, 6)
    for axis_at, parts in cuts:
        steps = jnp.exp(jax.random.uniform(jax.random.fold_in(own, axis_at), (parts,), jnp.float32, smallest / len(cuts), top_value / len(cuts)))
        level = level * jnp.repeat(steps, shape[axis_at] // parts).reshape([-1 if axis == axis_at else 1 for axis in range(len(shape))])
    return level


def shared_out(own_key, own, number, rows, number_of, top, bound, lean):
    ranking = jax.random.permutation(own_key, number_of)
    crowded, usual = load_shares(number_of, rows * top, bound, lean, True), load_shares(number_of, rows * top, bound, lean, False)
    places = jnp.arange(number_of)

    def named(sizes, turn):
        used = int((sizes > 0).sum())
        fixed = max(1, used // 4)
        shifted = fixed + (places - fixed + turn * (used - fixed)) % max(1, number_of - fixed)
        return jnp.zeros((number_of,), jnp.int32).at[ranking[jnp.where(places < fixed, places, shifted)]].set(jnp.asarray(sizes, jnp.int32))

    sizes = jnp.where(number % 4 == 0, named(crowded, number // 4), named(usual, number - number // 4 - 1))
    mixed = jax.random.permutation(jax.random.fold_in(own, 3), number_of)
    giver, taker = mixed[0:number_of // 2 * 2:2], mixed[1:number_of // 2 * 2:2]
    slack = jnp.minimum(sizes[giver] - 1, bound - sizes[taker]) // 2
    slack = jnp.where((giver == ranking[0]) | (taker == ranking[0]) | (sizes[taker] == 0), 0, jnp.maximum(slack, 0))
    shifted = jax.random.randint(jax.random.fold_in(own, 4), (number_of // 2,), 0, 1 << 20) % (slack + 1)
    sizes = sizes.at[giver].add(-shifted).at[taker].add(shifted)
    items = jnp.searchsorted(jnp.cumsum(sizes), jnp.arange(rows * top), side="right").astype(jnp.int32)
    grid = items.reshape(top, rows).T
    grid = grid[jax.random.permutation(jax.random.fold_in(own, 1), rows)]
    turn = jax.random.randint(jax.random.fold_in(own, 2), (rows, 1), 0, top)
    return jnp.take_along_axis(grid, (jnp.arange(top)[None, :] + turn) % top, axis=1)


def load_shares(number_of, total, bound, lean, full):
    portions = [(1 << 20) // math.isqrt(standing ** lean) + 1 for standing in range(1, number_of + 1)]
    largest = bound if full else min(bound, max(-(-total // number_of), total * portions[0] // sum(portions)))
    least = 1 if total - largest >= number_of - 1 else 0
    counts, surplus = [largest] + [least] * (number_of - 1), total - largest - least * (number_of - 1)
    while surplus > 0:
        free = [i for i in range(1, number_of) if counts[i] < largest] or [i for i in range(1, number_of) if counts[i] < bound]
        mass, budget = sum([portions[i] for i in free]), surplus
        for i in free:
            more = min(bound - counts[i], max(1, budget * portions[i] // mass), surplus)
            counts[i] = counts[i] + more
            surplus = surplus - more
    return np.array(counts)


def bell_draw(key, extent, deviation, reach, cuts=(), kind=jnp.bfloat16):
    entries = jax.random.normal(key, extent, jnp.float32) * deviation
    if len(cuts) > 0:
        entries = level_of(key, extent, cuts, -0.22, 0.18) * entries
    return jnp.clip(entries, min=-reach, max=reach).astype(kind)


def setup_inputs(seed: int = 0, part: int = 0) -> dict:
    arg_keys = jax.random.split(jax.random.key(seed), 14)
    own_keys = jax.random.split(jax.random.fold_in(arg_keys[13], part), 14)
    tokens = bell_draw(own_keys[0], (TOKENS, D), 1.0, 6.0, ((0, 16),))
    out_grad = bell_draw(own_keys[1], (TOKENS, D), 1.0, 6.0, ((0, 16),))
    routes_keys = jax.random.split(jax.random.fold_in(own_keys[2], 1), TOKENS // TOK_DEV)
    routes_turns = jax.random.permutation(jax.random.fold_in(own_keys[2], 3), TOKENS // TOK_DEV)
    routes = jax.vmap(lambda own, number: shared_out(jax.random.fold_in(own_keys[2], 2), own, number, TOK_DEV, EXPERTS, TOP, CAP, 2))(routes_keys, routes_turns).reshape((TOKENS, TOP))
    route_weights = jnp.clip(0.049804688 + 0.24902344 * jax.random.uniform(own_keys[3], (TOKENS, TOP), jnp.float32) ** level_of(own_keys[3], (TOKENS, TOP), ((0, 16),), -0.2, 0.2), 0.049804688, 0.29882812).astype(jnp.bfloat16)
    gate_weight = bell_draw(arg_keys[4], (EXPERTS, D, H), D ** -0.5, 0.125, ((0, 16),))
    up_weight = bell_draw(arg_keys[5], (EXPERTS, D, H), D ** -0.5, 0.125, ((0, 16),))
    down_weight = bell_draw(arg_keys[6], (EXPERTS, H, D), H ** -0.5, 0.21875, ((0, 16),))
    gate_adapter_input = bell_draw(arg_keys[7], (EXPERTS, R, D), D ** -0.5, 0.125, ((0, 16),))
    gate_adapter_output = bell_draw(arg_keys[8], (EXPERTS, R, H), R ** -0.5, 1.5, ((0, 16),))
    up_adapter_input = bell_draw(arg_keys[9], (EXPERTS, R, D), D ** -0.5, 0.125, ((0, 16),))
    up_adapter_output = bell_draw(arg_keys[10], (EXPERTS, R, H), R ** -0.5, 1.5, ((0, 16),))
    down_adapter_input = bell_draw(arg_keys[11], (EXPERTS, R, H), H ** -0.5, 0.21875, ((0, 16),))
    down_adapter_output = bell_draw(arg_keys[12], (EXPERTS, R, D), R ** -0.5, 1.5, ((0, 16),))
    return dict(tokens=tokens, out_grad=out_grad, routes=routes, route_weights=route_weights, gate_weight=gate_weight, up_weight=up_weight, down_weight=down_weight, gate_adapter_input=gate_adapter_input, gate_adapter_output=gate_adapter_output, up_adapter_input=up_adapter_input, up_adapter_output=up_adapter_output, down_adapter_input=down_adapter_input, down_adapter_output=down_adapter_output)


ADAPTER_SCALING = 0.5


def slot_ranks(id_block, expert_count):
    flat_ids = id_block.reshape(-1)
    one_hot = (flat_ids[:, None] == jnp.arange(expert_count, dtype=jnp.int32)[None, :]).astype(jnp.int32)
    earlier = jnp.cumsum(one_hot, 0) - one_hot
    return jnp.sum(earlier * one_hot, 1).astype(jnp.int32).reshape(id_block.shape)


def low_rank(factor_matrix, multiplier):
    return lax.dot_general(factor_matrix, multiplier, (((1,), (1,)), ((), ())), preferred_element_type=jnp.float32).astype(jnp.bfloat16)


def outer_sum(factor_matrix, multiplier):
    return ADAPTER_SCALING * lax.dot_general(factor_matrix, multiplier, (((0,), (0,)), ((), ())), preferred_element_type=jnp.float32)


def expert_backward(input_rows, rows_grad, rows_weight, gate_weight, up_weight, down_weight, gate_adapter_input, gate_adapter_output, up_adapter_input, up_adapter_output, down_adapter_input, down_adapter_output):
    gate_reduced = low_rank(input_rows, gate_adapter_input)
    up_reduced = low_rank(input_rows, up_adapter_input)
    gate_preactivation = jnp.dot(input_rows, gate_weight, preferred_element_type=jnp.float32) + ADAPTER_SCALING * jnp.dot(gate_reduced, gate_adapter_output, preferred_element_type=jnp.float32)
    up_preactivation = jnp.dot(input_rows, up_weight, preferred_element_type=jnp.float32) + ADAPTER_SCALING * jnp.dot(up_reduced, up_adapter_output, preferred_element_type=jnp.float32)
    sigmoid_gate = jax.nn.sigmoid(gate_preactivation)
    activated = gate_preactivation * sigmoid_gate
    hidden_state = (activated * up_preactivation).astype(jnp.bfloat16)
    hidden_reduced = low_rank(hidden_state, down_adapter_input)
    expert_result = (jnp.dot(hidden_state, down_weight, preferred_element_type=jnp.float32) + ADAPTER_SCALING * jnp.dot(hidden_reduced, down_adapter_output, preferred_element_type=jnp.float32)).astype(jnp.bfloat16)
    position_gradient = (rows_weight.astype(jnp.float32)[:, None] * rows_grad.astype(jnp.float32)).astype(jnp.bfloat16)
    reduced_gradient = low_rank(position_gradient, down_adapter_output)
    hidden_gradient = lax.dot_general(position_gradient, down_weight, (((1,), (1,)), ((), ())), preferred_element_type=jnp.float32) + ADAPTER_SCALING * jnp.dot(reduced_gradient, down_adapter_input, preferred_element_type=jnp.float32)
    grad_gate = (hidden_gradient * up_preactivation * sigmoid_gate * (1.0 + gate_preactivation * (1.0 - sigmoid_gate))).astype(jnp.bfloat16)
    grad_up = (hidden_gradient * activated).astype(jnp.bfloat16)
    gate_reduced_gradient = low_rank(grad_gate, gate_adapter_output)
    up_reduced_gradient = low_rank(grad_up, up_adapter_output)
    gradient_rows = lax.dot_general(grad_gate, gate_weight, (((1,), (1,)), ((), ())), preferred_element_type=jnp.float32)
    gradient_rows = gradient_rows + lax.dot_general(grad_up, up_weight, (((1,), (1,)), ((), ())), preferred_element_type=jnp.float32)
    gradient_rows = gradient_rows + ADAPTER_SCALING * (jnp.dot(gate_reduced_gradient, gate_adapter_input, preferred_element_type=jnp.float32) + jnp.dot(up_reduced_gradient, up_adapter_input, preferred_element_type=jnp.float32))
    adapter_grads = (outer_sum(gate_reduced_gradient, input_rows), outer_sum(gate_reduced, grad_gate), outer_sum(up_reduced_gradient, input_rows), outer_sum(up_reduced, grad_up), outer_sum(reduced_gradient, hidden_state), outer_sum(hidden_reduced, position_gradient))
    return gradient_rows.astype(jnp.bfloat16), expert_result, adapter_grads


def reference(tokens, out_grad, routes, route_weights, gate_weight, up_weight, down_weight, gate_adapter_input, gate_adapter_output, up_adapter_input, up_adapter_output, down_adapter_input, down_adapter_output):
    expert_rows = N_EXPERT * CAP
    id_blocks = routes.reshape(N_EXPERT, TOK_DEV, TOP)
    ranks = jax.vmap(lambda block: slot_ranks(block, EXPERTS))(id_blocks)
    source = jnp.arange(N_EXPERT, dtype=jnp.int32)[:, None, None]
    targets = (id_blocks * expert_rows + source * CAP + ranks).astype(jnp.int32).reshape(-1)
    token_index = jnp.repeat(jnp.arange(TOKENS, dtype=jnp.int32), TOP)
    table = jnp.full((EXPERTS * expert_rows,), TOKENS, jnp.int32).at[targets].set(token_index)
    weight_table = jnp.zeros((EXPERTS * expert_rows,), jnp.bfloat16).at[targets].set(route_weights.reshape(-1))
    tokens_padded = jnp.concatenate([tokens, jnp.zeros((1, D), jnp.bfloat16)], 0)
    grads_padded = jnp.concatenate([out_grad, jnp.zeros((1, D), jnp.bfloat16)], 0)
    input_rows = tokens_padded[table].reshape(EXPERTS, expert_rows, D)
    rows_grad = grads_padded[table].reshape(EXPERTS, expert_rows, D)
    rows_weight = weight_table.reshape(EXPERTS, expert_rows)

    def one_expert(pieces):
        return expert_backward(*pieces)

    gradient_rows, expert_result, adapter_grads = lax.map(one_expert, (input_rows, rows_grad, rows_weight, gate_weight, up_weight, down_weight, gate_adapter_input, gate_adapter_output, up_adapter_input, up_adapter_output, down_adapter_input, down_adapter_output))
    routed = gradient_rows.reshape(-1, D)[targets].reshape(TOKENS, TOP, D).astype(jnp.float32)
    grad_tokens = jnp.sum(routed, 1).astype(jnp.bfloat16)
    outputs = expert_result.reshape(-1, D)[targets].reshape(TOKENS, TOP, D).astype(jnp.float32)
    grad_weights = jnp.sum(out_grad.astype(jnp.float32)[:, None, :] * outputs, -1)
    return (grad_tokens, grad_weights, adapter_grads[0], adapter_grads[1], adapter_grads[2], adapter_grads[3], adapter_grads[4], adapter_grads[5])
```

```python
import jax
import jax.numpy as jnp
from jax import lax
from jax.sharding import PartitionSpec as P

ADAPTER_SCALING = 0.5


def slot_ranks(id_block, expert_count):
    flat_ids = id_block.reshape(-1)
    one_hot = (flat_ids[:, None] == jnp.arange(expert_count, dtype=jnp.int32)[None, :]).astype(
        jnp.int32
    )
    earlier = jnp.cumsum(one_hot, 0) - one_hot
    return jnp.sum(earlier * one_hot, 1).reshape(id_block.shape)


def low_rank(factor_matrix, multiplier):
    return lax.dot_general(
        factor_matrix, multiplier, (((1,), (1,)), ((), ())), preferred_element_type=jnp.float32
    ).astype(jnp.bfloat16)


def outer_sum(factor_matrix, multiplier):
    return ADAPTER_SCALING * lax.dot_general(
        factor_matrix, multiplier, (((0,), (0,)), ((), ())), preferred_element_type=jnp.float32
    )


def expert_backward(
    input_rows,
    rows_grad,
    rows_weight,
    gate_weight,
    up_weight,
    down_weight,
    gate_adapter_input,
    gate_adapter_output,
    up_adapter_input,
    up_adapter_output,
    down_adapter_input,
    down_adapter_output,
):
    gate_reduced = low_rank(input_rows, gate_adapter_input)
    up_reduced = low_rank(input_rows, up_adapter_input)
    gate_preactivation = jnp.dot(
        input_rows, gate_weight, preferred_element_type=jnp.float32
    ) + ADAPTER_SCALING * jnp.dot(
        gate_reduced, gate_adapter_output, preferred_element_type=jnp.float32
    )
    up_preactivation = jnp.dot(
        input_rows, up_weight, preferred_element_type=jnp.float32
    ) + ADAPTER_SCALING * jnp.dot(up_reduced, up_adapter_output, preferred_element_type=jnp.float32)
    sigmoid_gate = jax.nn.sigmoid(gate_preactivation)
    activated = gate_preactivation * sigmoid_gate
    hidden_state = (activated * up_preactivation).astype(jnp.bfloat16)
    hidden_reduced = low_rank(hidden_state, down_adapter_input)
    expert_result = (
        jnp.dot(hidden_state, down_weight, preferred_element_type=jnp.float32)
        + ADAPTER_SCALING
        * jnp.dot(hidden_reduced, down_adapter_output, preferred_element_type=jnp.float32)
    ).astype(jnp.bfloat16)
    position_gradient = (
        rows_weight.astype(jnp.float32)[:, None] * rows_grad.astype(jnp.float32)
    ).astype(jnp.bfloat16)
    reduced_gradient = low_rank(position_gradient, down_adapter_output)
    hidden_gradient = lax.dot_general(
        position_gradient, down_weight, (((1,), (1,)), ((), ())), preferred_element_type=jnp.float32
    ) + ADAPTER_SCALING * jnp.dot(
        reduced_gradient, down_adapter_input, preferred_element_type=jnp.float32
    )
    grad_gate = (
        hidden_gradient
        * up_preactivation
        * sigmoid_gate
        * (1.0 + gate_preactivation * (1.0 - sigmoid_gate))
    ).astype(jnp.bfloat16)
    grad_up = (hidden_gradient * activated).astype(jnp.bfloat16)
    gate_reduced_gradient = low_rank(grad_gate, gate_adapter_output)
    up_reduced_gradient = low_rank(grad_up, up_adapter_output)
    gradient_rows = lax.dot_general(
        grad_gate, gate_weight, (((1,), (1,)), ((), ())), preferred_element_type=jnp.float32
    )
    gradient_rows = gradient_rows + lax.dot_general(
        grad_up, up_weight, (((1,), (1,)), ((), ())), preferred_element_type=jnp.float32
    )
    gradient_rows = gradient_rows + ADAPTER_SCALING * (
        jnp.dot(gate_reduced_gradient, gate_adapter_input, preferred_element_type=jnp.float32)
        + jnp.dot(up_reduced_gradient, up_adapter_input, preferred_element_type=jnp.float32)
    )
    adapter_grads = (
        outer_sum(gate_reduced_gradient, input_rows),
        outer_sum(gate_reduced, grad_gate),
        outer_sum(up_reduced_gradient, input_rows),
        outer_sum(up_reduced, grad_up),
        outer_sum(reduced_gradient, hidden_state),
        outer_sum(hidden_reduced, position_gradient),
    )
    return (gradient_rows.astype(jnp.bfloat16), expert_result, adapter_grads)


def shards(
    tokens,
    out_grad,
    routes,
    route_weights,
    gate_weight,
    up_weight,
    down_weight,
    gate_adapter_input,
    gate_adapter_output,
    up_adapter_input,
    up_adapter_output,
    down_adapter_input,
    down_adapter_output,
):
    tok_rows, features = tokens.shape
    top_count = routes.shape[1]
    peer_count = lax.axis_size("expert")
    experts = peer_count * gate_weight.shape[0]
    capacity = tok_rows * top_count * 5 // (4 * experts)
    targets = routes * capacity + slot_ranks(routes, experts)
    matches = jnp.arange(experts * capacity, dtype=jnp.int32)[:, None, None] == targets[None, :, :]
    placing = jnp.any(matches, -1).astype(jnp.bfloat16)
    slot_weight = jnp.sum(
        jnp.where(matches, route_weights.astype(jnp.float32)[None, :, :], 0.0), (1, 2)
    ).astype(jnp.bfloat16)
    sent_rows = jnp.dot(placing, tokens, preferred_element_type=jnp.float32).astype(jnp.bfloat16)
    sent_grads = jnp.dot(placing, out_grad, preferred_element_type=jnp.float32).astype(jnp.bfloat16)
    got_rows, got_grads, got_weight = (
        lax.all_to_all(
            sent_rows.reshape(experts, capacity, features),
            "expert",
            split_axis=0,
            concat_axis=0,
            tiled=True,
        ),
        lax.all_to_all(
            sent_grads.reshape(experts, capacity, features),
            "expert",
            split_axis=0,
            concat_axis=0,
            tiled=True,
        ),
        lax.all_to_all(
            slot_weight.reshape(experts, capacity),
            "expert",
            split_axis=0,
            concat_axis=0,
            tiled=True,
        ),
    )
    gradient_rows, expert_result, adapter_grads = expert_backward(
        got_rows.reshape(-1, features),
        got_grads.reshape(-1, features),
        got_weight.reshape(-1),
        gate_weight[0],
        up_weight[0],
        down_weight[0],
        gate_adapter_input[0],
        gate_adapter_output[0],
        up_adapter_input[0],
        up_adapter_output[0],
        down_adapter_input[0],
        down_adapter_output[0],
    )
    dots_here = jnp.sum(
        got_grads.reshape(-1, features).astype(jnp.float32) * expert_result.astype(jnp.float32), -1
    )
    back_rows = lax.all_to_all(
        gradient_rows.reshape(peer_count, capacity, features),
        "expert",
        split_axis=0,
        concat_axis=0,
        tiled=True,
    )
    slot_dots = lax.all_to_all(
        dots_here.reshape(peer_count, capacity), "expert", split_axis=0, concat_axis=0, tiled=True
    ).reshape(-1)
    grad_tokens = lax.dot_general(
        placing,
        back_rows.reshape(-1, features),
        (((0,), (0,)), ((), ())),
        preferred_element_type=jnp.float32,
    ).astype(jnp.bfloat16)
    grad_weights = jnp.take(slot_dots, targets.reshape(-1)).reshape(tok_rows, top_count)
    return (
        grad_tokens,
        grad_weights,
        adapter_grads[0][None],
        adapter_grads[1][None],
        adapter_grads[2][None],
        adapter_grads[3][None],
        adapter_grads[4][None],
        adapter_grads[5][None],
    )


def gathered_shards(
    tokens,
    out_grad,
    routes,
    route_weights,
    *expert_matrices,
):
    peer_count = lax.axis_size("expert")
    tok_rows = tokens.shape[0]
    experts = peer_count * expert_matrices[0].shape[0]
    chosen = routes[:, :, None] == jnp.arange(experts, dtype=jnp.int32)[None, None, :]
    weight_table = jnp.sum(
        jnp.where(chosen, route_weights.astype(jnp.float32)[:, :, None], 0.0), 1
    ).astype(jnp.bfloat16)
    all_rows = lax.all_gather(tokens, "expert", axis=0, tiled=True)
    all_grads = lax.all_gather(out_grad, "expert", axis=0, tiled=True)
    all_weights = lax.all_gather(weight_table, "expert", axis=0, tiled=True)
    own = jnp.arange(experts, dtype=jnp.int32)[None, :] == lax.axis_index("expert")
    own_weight = jnp.sum(
        jnp.where(own, all_weights.astype(jnp.float32), 0.0), 1
    ).astype(jnp.bfloat16)
    gradient_rows, expert_result, adapter_grads = expert_backward(
        all_rows, all_grads, own_weight, *[matrix[0] for matrix in expert_matrices]
    )
    dots_here = jnp.sum(all_grads.astype(jnp.float32) * expert_result.astype(jnp.float32), -1)
    grad_tokens = lax.psum_scatter(gradient_rows, "expert", scatter_dimension=0, tiled=True)
    token_dots = lax.all_to_all(
        dots_here.reshape(peer_count, tok_rows), "expert", split_axis=0, concat_axis=0, tiled=True
    )
    grad_weights = jnp.sum(jnp.where(chosen, token_dots.T[:, None, :], 0.0), 2)
    return (grad_tokens, grad_weights) + tuple(grad[None] for grad in adapter_grads)


def solution(mesh):
    return jax.shard_map(
        gathered_shards if mesh.shape["expert"] <= 16 else shards,
        mesh=mesh,
        in_specs=(
            P(("groups", "expert"), None),
            P(("groups", "expert"), None),
            P(("groups", "expert"), None),
            P(("groups", "expert"), None),
            P("expert", None, None),
            P("expert", None, None),
            P("expert", None, None),
            P("expert", None, None),
            P("expert", None, None),
            P("expert", None, None),
            P("expert", None, None),
            P("expert", None, None),
            P("expert", None, None),
        ),
        out_specs=(
            P(("groups", "expert"), None),
            P(("groups", "expert"), None),
            P(("groups", "expert"), None, None),
            P(("groups", "expert"), None, None),
            P(("groups", "expert"), None, None),
            P(("groups", "expert"), None, None),
            P(("groups", "expert"), None, None),
            P(("groups", "expert"), None, None),
        ),
        check_vma=False,
    )
```

```python
import jax
import jax.numpy as jnp
from jax import lax
from jax.experimental import pallas as pl
from jax.experimental.pallas import tpu as pltpu
from jax.sharding import PartitionSpec as P

ADAPTER_SCALING = 0.5
LANES = 128
PIECES = 4
SIB, SIDE, UP, DOWN = 0, 1, 2, 3
F32, BF16 = jnp.float32, jnp.bfloat16


def mm(a, b):
    return jnp.dot(a, b, preferred_element_type=F32)


def mm_t(a, b):
    return lax.dot_general(a, b, (((1,), (1,)), ((), ())), preferred_element_type=F32)


def turned(value):
    return value.astype(F32).T.astype(BF16)


def routed_kernel(
    x_ref, g_ref, routes_ref, weights_ref, wg, wu, wd, gin, gout, uin, uout, din, dout,
    tok_out, rw_out, ag_out, bg_out, au_out, bu_out, ad_out, bd_out,
    xbuf, gbuf, part, sbuf, ybuf, zbuf,
    ain, aout, dinp, doutp, gate_s, up_s, gh_s, hid_s, gg_s, gu_s, low_s, hlow_s, wcol_s,
    acc_a, acc_b, acc_ad, acc_bd, total_s,
    xs, xr, gs, gr, ss, sr, ys, yr, zs, zr,
):
    rows, feat = x_ref.shape
    rank, hid = gout.shape
    plane_rows = 4 * rows
    piece = rows // PIECES
    me = lax.axis_index("expert")
    z, y, c = me // 4, (me // 2) % 2, me % 2
    half = z // 2
    inner = (z % 3 + 1) // 2
    target = {SIB: me + 1 - 2 * c, SIDE: me + 2 - 4 * y, UP: (me + 4) % 16, DOWN: (me + 12) % 16}

    def plane_at(s):
        p = s + inner * (1 - s // 2) * (1 - 2 * s)
        return p + half * (3 - 2 * p)

    def block(p, yy, cc):
        return p * 4 + yy * 2 + cc

    def remote(src, dst, send, recv, kind):
        return pltpu.make_async_remote_copy(
            src_ref=src, dst_ref=dst, send_sem=send, recv_sem=recv,
            device_id={"expert": target[kind]}, device_id_type=pl.DeviceIdType.MESH,
        )

    barrier = pltpu.get_barrier_semaphore()

    def greet(kind):
        pl.semaphore_signal(
            barrier, inc=1, device_id={"expert": target[kind]},
            device_id_type=pl.DeviceIdType.MESH,
        )

    greet(SIB)
    greet(SIDE)
    pl.when(z < 3)(lambda: greet(UP))
    pl.when(z > 0)(lambda: greet(DOWN))

    own = pl.ds(me * rows, rows)
    xbuf[own, :] = x_ref[...]
    gbuf[own, 0:feat] = g_ref[...]
    lane = lax.broadcasted_iota(jnp.int32, (rows, LANES), 1)
    route = routes_ref[...]
    route_w = weights_ref[...].astype(F32)
    table = jnp.zeros((rows, LANES), F32)
    for k in range(route.shape[1]):
        table = jnp.where(lane == route[:, k : k + 1], route_w[:, k : k + 1], table)
    gbuf[own, feat:] = table.astype(BF16)

    pl.semaphore_wait(barrier, 3 + inner)

    def wide(buf, send, recv, kind, b):
        at = buf.at[pl.ds(b * rows, rows)]
        return remote(at, at, send.at[kind, b], recv.at[b], kind)

    arrays = ((xbuf, xs, xr), (gbuf, gs, gr))

    def each_own(arr, act):
        act(wide(*arr, SIDE, me))
        pl.when(z < 3)(lambda: act(wide(*arr, UP, me)))
        pl.when(z > 0)(lambda: act(wide(*arr, DOWN, me)))
        act(wide(*arr, SIB, me))

    def each_column(arr, p, act):
        b = block(p, y, c)
        pl.when(jnp.logical_and(p < z, z < 3))(lambda: act(wide(*arr, UP, b)))
        pl.when(jnp.logical_and(p > z, z > 0))(lambda: act(wide(*arr, DOWN, b)))
        act(wide(*arr, SIDE, b))
        act(wide(*arr, SIB, b))

    def start(copy):
        copy.start()

    def relay_z(arr, p):
        wide(*arr, SIB, block(p, y, c)).wait_recv()
        each_column(arr, p, start)

    def relay_y(arr, p):
        b = block(p, 1 - y, c)
        wide(*arr, SIB, b).wait_recv()
        wide(*arr, SIB, b).start()

    def wait_sib(arr, p):
        wide(*arr, SIB, block(p, 0, 1 - c)).wait_recv()
        wide(*arr, SIB, block(p, 1, 1 - c)).wait_recv()

    def relays(arr, s):
        relay_y(arr, plane_at(s))

        @pl.when(s < 3 - inner)
        def _():
            relay_z(arr, plane_at(s + 1 + inner * s))

        @pl.when(jnp.logical_and(inner == 1, s == 0))
        def _():
            relay_z(arr, plane_at(2))

    for arr in arrays:
        each_own(arr, start)

    ain[...] = jnp.zeros_like(ain)
    aout[...] = jnp.zeros_like(aout)
    dinp[...] = jnp.zeros_like(dinp)
    doutp[...] = jnp.zeros_like(doutp)
    ain[0:rank, :] = gin[...]
    ain[rank : 2 * rank, :] = uin[...]
    aout[0:rank, 0:hid] = gout[...]
    aout[rank : 2 * rank, hid:] = uout[...]
    dinp[0:rank, :] = din[...]
    doutp[0:rank, :] = dout[...]
    acc_a[...] = jnp.zeros_like(acc_a)
    acc_b[...] = jnp.zeros_like(acc_b)
    acc_ad[...] = jnp.zeros_like(acc_ad)
    acc_bd[...] = jnp.zeros_like(acc_bd)

    def to_sib(p, yy):
        return remote(
            part.at[pl.ds(block(p, yy, 1 - c) * rows, rows)],
            sbuf.at[pl.ds((p * 2 + yy) * rows, rows)],
            ss.at[p * 2 + yy], sr.at[p * 2 + yy], SIB,
        )

    def to_side(p, h):
        return remote(
            sbuf.at[pl.ds((p * 2 + 1 - y) * rows + h * piece, piece)],
            ybuf.at[pl.ds(p * rows + h * piece, piece)],
            ys.at[p, h], yr.at[p, h], SIDE,
        )

    def along(p, h, kind):
        lead = 0 if kind == UP else 1
        return remote(
            ybuf.at[pl.ds(p * rows + h * piece, piece)],
            zbuf.at[lead, pl.ds(p * rows + h * piece, piece)],
            zs.at[p, h], zr.at[lead, p, h], kind,
        )

    def sum_sib(p):
        to_sib(p, 1 - y).wait_recv()

        def step(h, _):
            at = pl.ds((p * 2 + 1 - y) * rows + h * piece, piece)
            mine = pl.ds(block(p, 1 - y, c) * rows + h * piece, piece)
            sbuf[at, :] = (sbuf[at, :].astype(F32) + part[mine, :].astype(F32)).astype(BF16)
            to_side(p, h).start()
            return 0

        lax.fori_loop(0, PIECES, step, 0)
        to_sib(p, y).wait_recv()

    def pair_sum(p, h):
        to_side(p, h).wait_recv()
        here = pl.ds(block(p, y, c) * rows + h * piece, piece)
        near = pl.ds((p * 2 + y) * rows + h * piece, piece)
        at = pl.ds(p * rows + h * piece, piece)
        return part[here, :].astype(F32) + sbuf[near, :].astype(F32) + ybuf[at, :].astype(F32)

    def pass_on(p, h):
        at = pl.ds(p * rows + h * piece, piece)
        ybuf[at, :] = pair_sum(p, h).astype(BF16)

        @pl.when(p > z)
        def _():
            @pl.when(z > 0)
            def _():
                along(p, h, UP).wait_recv()
                ybuf[at, :] = (ybuf[at, :].astype(F32) + zbuf[0, at, :].astype(F32)).astype(BF16)

            along(p, h, UP).start()

        @pl.when(p < z)
        def _():
            @pl.when(z < 3)
            def _():
                along(p, h, DOWN).wait_recv()
                ybuf[at, :] = (ybuf[at, :].astype(F32) + zbuf[1, at, :].astype(F32)).astype(BF16)

            along(p, h, DOWN).start()

    def pass_all(p):
        def step(h, _):
            pass_on(p, h)
            return 0

        lax.fori_loop(0, PIECES, step, 0)

    chunk = 16
    expert_lane = lax.broadcasted_iota(jnp.int32, (chunk, LANES), 1)

    def forward(p):
        at = pl.ds(p * plane_rows, plane_rows)
        x = xbuf[at, :]
        low = mm_t(x, ain[...]).astype(BF16)
        low_s[...] = low
        gate_s[...] = mm(x, wg[...]) + ADAPTER_SCALING * mm(low, aout[:, 0:hid])
        up_s[...] = mm(x, wu[...]) + ADAPTER_SCALING * mm(low, aout[:, hid:])

        def step(r, _):
            rr = pl.ds(r * chunk, chunk)
            gate = gate_s[rr, :]
            act = gate * jax.nn.sigmoid(gate)
            hid_s[rr, :] = (act * up_s[rr, :]).astype(BF16)
            return 0

        lax.fori_loop(0, plane_rows // chunk, step, 0)
        hlow_s[...] = mm_t(hid_s[...], dinp[...])

    def backward(p):
        at = pl.ds(p * plane_rows, plane_rows)
        g = gbuf[at, 0:feat]
        glow = mm_t(g, doutp[...])
        gh_s[...] = mm_t(g, wd[...]) + ADAPTER_SCALING * mm(glow.astype(BF16), dinp[...])

        def step(r, _):
            rr = pl.ds(r * chunk, chunk)
            full = pl.ds(p * plane_rows + r * chunk, chunk)
            gh = gh_s[rr, :]
            gate = gate_s[rr, :]
            up = up_s[rr, :]
            sig = jax.nn.sigmoid(gate)
            act = gate * sig
            w = jnp.sum(
                jnp.where(expert_lane == me, gbuf[full, feat:].astype(F32), 0.0), 1, keepdims=True
            )
            wcol_s[rr, :] = jnp.broadcast_to(w, (chunk, LANES))
            dots = jnp.sum(hid_s[rr, :].astype(F32) * gh, 1, keepdims=True)
            high = dots.astype(BF16).astype(F32)
            part[full, feat:] = jnp.where(
                expert_lane == me, high, jnp.where(expert_lane == me + 16, dots - high, 0.0)
            ).astype(BF16)
            gh = gh * w
            gg_s[rr, :] = (gh * up * sig * (1.0 + gate * (1.0 - sig))).astype(BF16)
            gu_s[rr, :] = (gh * act).astype(BF16)
            return 0

        lax.fori_loop(0, plane_rows // chunk, step, 0)
        gg, gu = gg_s[...], gu_s[...]
        lg = (mm_t(gg, aout[:, 0:hid]) + mm_t(gu, aout[:, hid:])).astype(BF16)
        wide_n = min(512, feat)
        for n in range(0, feat, wide_n):
            cols = slice(n, n + wide_n)
            part[at, cols] = (
                mm_t(gg, wg[cols, :])
                + mm_t(gu, wu[cols, :])
                + ADAPTER_SCALING * mm(lg, ain[:, cols])
            ).astype(BF16)
        return glow, lg

    def outer(p, glow, lg):
        at = pl.ds(p * plane_rows, plane_rows)
        w = wcol_s[...]
        acc_a[...] += mm(turned(lg)[0 : 2 * rank], xbuf[at, :])
        low_t = turned(low_s[...])[0 : 2 * rank]
        acc_b[:, 0:hid] += mm(low_t, gg_s[...])
        acc_b[:, hid:] += mm(low_t, gu_s[...])
        acc_ad[...] += mm(turned(w * glow)[0:rank], hid_s[...])
        hlow = hlow_s[...].astype(BF16).astype(F32)
        acc_bd[...] += mm(turned(w * hlow)[0:rank], gbuf[at, 0:feat])

    def body(s, _):
        p = plane_at(s)
        before = plane_at(jnp.maximum(s - 1, 0))
        relays(arrays[0], s)
        wait_sib(arrays[0], p)
        forward(p)
        pl.when(s >= 1)(lambda: sum_sib(before))
        relays(arrays[1], s)
        wait_sib(arrays[1], p)
        glow, lg = backward(p)
        to_sib(p, 0).start()
        to_sib(p, 1).start()
        outer(p, glow, lg)
        pl.when(s >= 2 + inner)(lambda: pass_all(before))
        return 0

    lax.fori_loop(0, 4, body, 0)
    last = plane_at(3)
    sum_sib(last)

    def tail(h, _):
        pass_on(last, h)
        pl.when(inner == 1)(lambda: pass_on(plane_at(1), h))
        return 0

    lax.fori_loop(0, PIECES, tail, 0)

    ag_out[...] = ADAPTER_SCALING * acc_a[0:rank, :]
    au_out[...] = ADAPTER_SCALING * acc_a[rank : 2 * rank, :]
    bg_out[...] = ADAPTER_SCALING * acc_b[0:rank, 0:hid]
    bu_out[...] = ADAPTER_SCALING * acc_b[rank : 2 * rank, hid:]
    ad_out[...] = ADAPTER_SCALING * acc_ad[...]
    bd_out[...] = ADAPTER_SCALING * acc_bd[...]

    def finish(h, _):
        at = pl.ds(z * rows + h * piece, piece)
        total_s[...] = pair_sum(z, h)

        @pl.when(z > 0)
        def _():
            along(z, h, UP).wait_recv()
            total_s[...] += zbuf[0, at, :].astype(F32)

        @pl.when(z < 3)
        def _():
            along(z, h, DOWN).wait_recv()
            total_s[...] += zbuf[1, at, :].astype(F32)

        ybuf[at, :] = total_s[...].astype(BF16)
        return 0

    lax.fori_loop(0, PIECES, finish, 0)
    at = pl.ds(z * rows, rows)
    tok_out[...] = ybuf[at, 0:feat]
    dots = ybuf[at, feat:].astype(F32)
    place = lax.broadcasted_iota(jnp.int32, route.shape, 1)
    result = jnp.zeros(route.shape, F32)
    for k in range(route.shape[1]):
        pick = jnp.logical_or(lane == route[:, k : k + 1], lane == route[:, k : k + 1] + 16)
        value = jnp.sum(jnp.where(pick, dots, 0.0), 1, keepdims=True)
        result = jnp.where(place == k, value, result)
    rw_out[...] = result

    def sent(copy):
        copy.wait_send()

    for arr in arrays:
        each_own(arr, sent)

        def settle(p, _):
            pl.when(p != z)(lambda: each_column(arr, p, sent))
            sent(wide(*arr, SIB, block(p, 1 - y, c)))
            return 0

        lax.fori_loop(0, 4, settle, 0)

    def settle_sums(p, _):
        sent(to_sib(p, 0))
        sent(to_sib(p, 1))

        def step(h, _):
            sent(to_side(p, h))
            pl.when(p > z)(lambda: sent(along(p, h, UP)))
            pl.when(p < z)(lambda: sent(along(p, h, DOWN)))
            return 0

        lax.fori_loop(0, PIECES, step, 0)
        return 0

    lax.fori_loop(0, 4, settle_sums, 0)


def kernel_shards(tokens, out_grad, routes, route_weights, *matrices):
    matrices = [matrix[0] for matrix in matrices]
    rows, feat = tokens.shape
    rank, hid = matrices[4].shape
    wide = feat + LANES
    plane = 4 * rows
    shape = jax.ShapeDtypeStruct
    vmem = pltpu.VMEM
    sem = pltpu.SemaphoreType.DMA
    outs = pl.pallas_call(
        routed_kernel,
        out_shape=(
            shape((rows, feat), BF16),
            shape(routes.shape, F32),
            shape((rank, feat), F32),
            shape((rank, hid), F32),
            shape((rank, feat), F32),
            shape((rank, hid), F32),
            shape((rank, hid), F32),
            shape((rank, feat), F32),
        ),
        in_specs=[pl.BlockSpec(memory_space=pltpu.VMEM)] * 13,
        out_specs=tuple([pl.BlockSpec(memory_space=pltpu.VMEM)] * 8),
        scratch_shapes=[
            vmem((16 * rows, feat), BF16),
            vmem((16 * rows, wide), BF16),
            vmem((16 * rows, wide), BF16),
            vmem((8 * rows, wide), BF16),
            vmem((4 * rows, wide), BF16),
            vmem((2, 4 * rows, wide), BF16),
            vmem((LANES, feat), BF16),
            vmem((LANES, 2 * hid), BF16),
            vmem((LANES, hid), BF16),
            vmem((LANES, feat), BF16),
            vmem((plane, hid), F32),
            vmem((plane, hid), F32),
            vmem((plane, hid), F32),
            vmem((plane, hid), BF16),
            vmem((plane, hid), BF16),
            vmem((plane, hid), BF16),
            vmem((plane, LANES), BF16),
            vmem((plane, LANES), F32),
            vmem((plane, LANES), F32),
            vmem((2 * rank, feat), F32),
            vmem((2 * rank, 2 * hid), F32),
            vmem((rank, hid), F32),
            vmem((rank, feat), F32),
            vmem((rows // PIECES, wide), F32),
            sem((4, 16)), sem((16,)), sem((4, 16)), sem((16,)),
            sem((8,)), sem((8,)),
            sem((4, PIECES)), sem((4, PIECES)),
            sem((4, PIECES)), sem((2, 4, PIECES)),
        ],
        compiler_params=pltpu.CompilerParams(
            collective_id=0, has_side_effects=True, vmem_limit_bytes=60 * 1024 * 1024
        ),
        cost_estimate=pl.CostEstimate(
            flops=12 * 16 * rows * feat * hid, bytes_accessed=6 * feat * hid + 8 * rows * feat,
            transcendentals=16 * rows * hid,
        ),
    )(tokens, out_grad, routes, route_weights, *matrices)
    return outs[:2] + tuple(out[None] for out in outs[2:])


def slot_ranks(id_block, expert_count):
    flat_ids = id_block.reshape(-1)
    one_hot = (flat_ids[:, None] == jnp.arange(expert_count, dtype=jnp.int32)[None, :]).astype(
        jnp.int32
    )
    earlier = jnp.cumsum(one_hot, 0) - one_hot
    return jnp.sum(earlier * one_hot, 1).reshape(id_block.shape)


def low_rank(factor_matrix, multiplier):
    return lax.dot_general(
        factor_matrix, multiplier, (((1,), (1,)), ((), ())), preferred_element_type=jnp.float32
    ).astype(jnp.bfloat16)


def outer_sum(factor_matrix, multiplier):
    return ADAPTER_SCALING * lax.dot_general(
        factor_matrix, multiplier, (((0,), (0,)), ((), ())), preferred_element_type=jnp.float32
    )


def expert_backward(
    input_rows,
    rows_grad,
    rows_weight,
    gate_weight,
    up_weight,
    down_weight,
    gate_adapter_input,
    gate_adapter_output,
    up_adapter_input,
    up_adapter_output,
    down_adapter_input,
    down_adapter_output,
):
    gate_reduced = low_rank(input_rows, gate_adapter_input)
    up_reduced = low_rank(input_rows, up_adapter_input)
    gate_preactivation = jnp.dot(
        input_rows, gate_weight, preferred_element_type=jnp.float32
    ) + ADAPTER_SCALING * jnp.dot(
        gate_reduced, gate_adapter_output, preferred_element_type=jnp.float32
    )
    up_preactivation = jnp.dot(
        input_rows, up_weight, preferred_element_type=jnp.float32
    ) + ADAPTER_SCALING * jnp.dot(up_reduced, up_adapter_output, preferred_element_type=jnp.float32)
    sigmoid_gate = jax.nn.sigmoid(gate_preactivation)
    activated = gate_preactivation * sigmoid_gate
    hidden_state = (activated * up_preactivation).astype(jnp.bfloat16)
    hidden_reduced = low_rank(hidden_state, down_adapter_input)
    expert_result = (
        jnp.dot(hidden_state, down_weight, preferred_element_type=jnp.float32)
        + ADAPTER_SCALING
        * jnp.dot(hidden_reduced, down_adapter_output, preferred_element_type=jnp.float32)
    ).astype(jnp.bfloat16)
    position_gradient = (
        rows_weight.astype(jnp.float32)[:, None] * rows_grad.astype(jnp.float32)
    ).astype(jnp.bfloat16)
    reduced_gradient = low_rank(position_gradient, down_adapter_output)
    hidden_gradient = lax.dot_general(
        position_gradient, down_weight, (((1,), (1,)), ((), ())), preferred_element_type=jnp.float32
    ) + ADAPTER_SCALING * jnp.dot(
        reduced_gradient, down_adapter_input, preferred_element_type=jnp.float32
    )
    grad_gate = (
        hidden_gradient
        * up_preactivation
        * sigmoid_gate
        * (1.0 + gate_preactivation * (1.0 - sigmoid_gate))
    ).astype(jnp.bfloat16)
    grad_up = (hidden_gradient * activated).astype(jnp.bfloat16)
    gate_reduced_gradient = low_rank(grad_gate, gate_adapter_output)
    up_reduced_gradient = low_rank(grad_up, up_adapter_output)
    gradient_rows = lax.dot_general(
        grad_gate, gate_weight, (((1,), (1,)), ((), ())), preferred_element_type=jnp.float32
    )
    gradient_rows = gradient_rows + lax.dot_general(
        grad_up, up_weight, (((1,), (1,)), ((), ())), preferred_element_type=jnp.float32
    )
    gradient_rows = gradient_rows + ADAPTER_SCALING * (
        jnp.dot(gate_reduced_gradient, gate_adapter_input, preferred_element_type=jnp.float32)
        + jnp.dot(up_reduced_gradient, up_adapter_input, preferred_element_type=jnp.float32)
    )
    adapter_grads = (
        outer_sum(gate_reduced_gradient, input_rows),
        outer_sum(gate_reduced, grad_gate),
        outer_sum(up_reduced_gradient, input_rows),
        outer_sum(up_reduced, grad_up),
        outer_sum(reduced_gradient, hidden_state),
        outer_sum(hidden_reduced, position_gradient),
    )
    return (gradient_rows.astype(jnp.bfloat16), expert_result, adapter_grads)


def shards(
    tokens,
    out_grad,
    routes,
    route_weights,
    gate_weight,
    up_weight,
    down_weight,
    gate_adapter_input,
    gate_adapter_output,
    up_adapter_input,
    up_adapter_output,
    down_adapter_input,
    down_adapter_output,
):
    tok_rows, features = tokens.shape
    top_count = routes.shape[1]
    peer_count = lax.axis_size("expert")
    experts = peer_count * gate_weight.shape[0]
    capacity = tok_rows * top_count * 5 // (4 * experts)
    targets = routes * capacity + slot_ranks(routes, experts)
    matches = jnp.arange(experts * capacity, dtype=jnp.int32)[:, None, None] == targets[None, :, :]
    placing = jnp.any(matches, -1).astype(jnp.bfloat16)
    slot_weight = jnp.sum(
        jnp.where(matches, route_weights.astype(jnp.float32)[None, :, :], 0.0), (1, 2)
    ).astype(jnp.bfloat16)
    sent_rows = jnp.dot(placing, tokens, preferred_element_type=jnp.float32).astype(jnp.bfloat16)
    sent_grads = jnp.dot(placing, out_grad, preferred_element_type=jnp.float32).astype(jnp.bfloat16)
    got_rows, got_grads, got_weight = (
        lax.all_to_all(
            sent_rows.reshape(experts, capacity, features),
            "expert",
            split_axis=0,
            concat_axis=0,
            tiled=True,
        ),
        lax.all_to_all(
            sent_grads.reshape(experts, capacity, features),
            "expert",
            split_axis=0,
            concat_axis=0,
            tiled=True,
        ),
        lax.all_to_all(
            slot_weight.reshape(experts, capacity),
            "expert",
            split_axis=0,
            concat_axis=0,
            tiled=True,
        ),
    )
    gradient_rows, expert_result, adapter_grads = expert_backward(
        got_rows.reshape(-1, features),
        got_grads.reshape(-1, features),
        got_weight.reshape(-1),
        gate_weight[0],
        up_weight[0],
        down_weight[0],
        gate_adapter_input[0],
        gate_adapter_output[0],
        up_adapter_input[0],
        up_adapter_output[0],
        down_adapter_input[0],
        down_adapter_output[0],
    )
    dots_here = jnp.sum(
        got_grads.reshape(-1, features).astype(jnp.float32) * expert_result.astype(jnp.float32), -1
    )
    back_rows = lax.all_to_all(
        gradient_rows.reshape(peer_count, capacity, features),
        "expert",
        split_axis=0,
        concat_axis=0,
        tiled=True,
    )
    slot_dots = lax.all_to_all(
        dots_here.reshape(peer_count, capacity), "expert", split_axis=0, concat_axis=0, tiled=True
    ).reshape(-1)
    grad_tokens = lax.dot_general(
        placing,
        back_rows.reshape(-1, features),
        (((0,), (0,)), ((), ())),
        preferred_element_type=jnp.float32,
    ).astype(jnp.bfloat16)
    grad_weights = jnp.take(slot_dots, targets.reshape(-1)).reshape(tok_rows, top_count)
    return (
        grad_tokens,
        grad_weights,
        adapter_grads[0][None],
        adapter_grads[1][None],
        adapter_grads[2][None],
        adapter_grads[3][None],
        adapter_grads[4][None],
        adapter_grads[5][None],
    )


def solution(mesh):
    return jax.shard_map(
        kernel_shards if mesh.shape["expert"] == 16 else shards,
        mesh=mesh,
        in_specs=(
            P(("groups", "expert"), None),
            P(("groups", "expert"), None),
            P(("groups", "expert"), None),
            P(("groups", "expert"), None),
            P("expert", None, None),
            P("expert", None, None),
            P("expert", None, None),
            P("expert", None, None),
            P("expert", None, None),
            P("expert", None, None),
            P("expert", None, None),
            P("expert", None, None),
            P("expert", None, None),
        ),
        out_specs=(
            P(("groups", "expert"), None),
            P(("groups", "expert"), None),
            P(("groups", "expert"), None, None),
            P(("groups", "expert"), None, None),
            P(("groups", "expert"), None, None),
            P(("groups", "expert"), None, None),
            P(("groups", "expert"), None, None),
            P(("groups", "expert"), None, None),
        ),
        check_vma=False,
    )
```

```python
import jax
import jax.numpy as jnp
from jax import lax
from jax.experimental import pallas as pl
from jax.experimental.pallas import tpu as pltpu
from jax.sharding import PartitionSpec as P

ADAPTER_SCALING = 0.5
LANES = 128
PIECES = 4
SIB, SIDE, UP, DOWN = 0, 1, 2, 3
F32, BF16 = jnp.float32, jnp.bfloat16


def mm(a, b):
    return jnp.dot(a, b, preferred_element_type=F32)


def mm_t(a, b):
    return lax.dot_general(a, b, (((1,), (1,)), ((), ())), preferred_element_type=F32)


def turned(value):
    return value.astype(F32).T.astype(BF16)


def routed_kernel(
    x_ref, g_ref, routes_ref, weights_ref, wg_far, wu_far, wd_far, gin, gout, uin, uout, din, dout,
    tok_out, rw_out, ag_out, bg_out, au_out, bu_out, ad_out, bd_out,
    xbuf, gbuf, part, sbuf, ybuf, zbuf,
    ain, aout, dinp, doutp, gate_s, up_s, gh_s, hid_s, gg_s, gu_s, low_s, hlow_s, wcol_s,
    acc_a, acc_b, acc_ad, acc_bd, total_s, wg, wu, wd, wsem,
    xs, xr, gs, gr, ss, sr, ys, yr, zs, zr,
):
    rows, feat = x_ref.shape
    rank, hid = gout.shape
    plane_rows = 4 * rows
    piece = rows // PIECES
    me = lax.axis_index("expert")
    z, y, c = me // 4, (me // 2) % 2, me % 2
    half = z // 2
    inner = (z % 3 + 1) // 2
    target = {SIB: me + 1 - 2 * c, SIDE: me + 2 - 4 * y, UP: (me + 4) % 16, DOWN: (me + 12) % 16}

    def plane_at(s):
        p = s + inner * (1 - s // 2) * (1 - 2 * s)
        return p + half * (3 - 2 * p)

    def block(p, yy, cc):
        return p * 4 + yy * 2 + cc

    def remote(src, dst, send, recv, kind):
        return pltpu.make_async_remote_copy(
            src_ref=src, dst_ref=dst, send_sem=send, recv_sem=recv,
            device_id={"expert": target[kind]}, device_id_type=pl.DeviceIdType.MESH,
        )

    barrier = pltpu.get_barrier_semaphore()

    def greet(kind):
        pl.semaphore_signal(
            barrier, inc=1, device_id={"expert": target[kind]},
            device_id_type=pl.DeviceIdType.MESH,
        )

    greet(SIB)
    greet(SIDE)
    pl.when(z < 3)(lambda: greet(UP))
    pl.when(z > 0)(lambda: greet(DOWN))

    own = pl.ds(me * rows, rows)
    xbuf[own, :] = x_ref[...]
    gbuf[own, 0:feat] = g_ref[...]
    lane = lax.broadcasted_iota(jnp.int32, (rows, LANES), 1)
    route = routes_ref[...].astype(F32).T.astype(jnp.int32)
    route_w = weights_ref[...].astype(F32).T
    table = jnp.zeros((rows, LANES), F32)
    for k in range(route.shape[1]):
        table = jnp.where(lane == route[:, k : k + 1], route_w[:, k : k + 1], table)
    gbuf[own, feat:] = table.astype(BF16)

    pl.semaphore_wait(barrier, 3 + inner)

    def wide(buf, send, recv, kind, b):
        at = buf.at[pl.ds(b * rows, rows)]
        return remote(at, at, send.at[kind, b], recv.at[b], kind)

    arrays = ((xbuf, xs, xr), (gbuf, gs, gr))

    def each_own(arr, act):
        act(wide(*arr, SIDE, me))
        pl.when(z < 3)(lambda: act(wide(*arr, UP, me)))
        pl.when(z > 0)(lambda: act(wide(*arr, DOWN, me)))
        act(wide(*arr, SIB, me))

    def each_column(arr, p, act):
        b = block(p, y, c)
        pl.when(jnp.logical_and(p < z, z < 3))(lambda: act(wide(*arr, UP, b)))
        pl.when(jnp.logical_and(p > z, z > 0))(lambda: act(wide(*arr, DOWN, b)))
        act(wide(*arr, SIDE, b))
        act(wide(*arr, SIB, b))

    def start(copy):
        copy.start()

    def relay_z(arr, p):
        wide(*arr, SIB, block(p, y, c)).wait_recv()
        each_column(arr, p, start)

    def relay_y(arr, p):
        b = block(p, 1 - y, c)
        wide(*arr, SIB, b).wait_recv()
        wide(*arr, SIB, b).start()

    def wait_sib(arr, p):
        wide(*arr, SIB, block(p, 0, 1 - c)).wait_recv()
        wide(*arr, SIB, block(p, 1, 1 - c)).wait_recv()

    def relays(arr, s):
        relay_y(arr, plane_at(s))

        @pl.when(s < 3 - inner)
        def _():
            relay_z(arr, plane_at(s + 1 + inner * s))

        @pl.when(jnp.logical_and(inner == 1, s == 0))
        def _():
            relay_z(arr, plane_at(2))

    for arr in arrays:
        each_own(arr, start)

    fetches = [
        pltpu.make_async_copy(far, near, wsem.at[at])
        for at, (far, near) in enumerate(((wg_far, wg), (wu_far, wu), (wd_far, wd)))
    ]
    for fetch in fetches:
        fetch.start()

    ain[...] = jnp.zeros_like(ain)
    aout[...] = jnp.zeros_like(aout)
    dinp[...] = jnp.zeros_like(dinp)
    doutp[...] = jnp.zeros_like(doutp)
    ain[0:rank, :] = gin[...]
    ain[rank : 2 * rank, :] = uin[...]
    aout[0:rank, 0:hid] = gout[...]
    aout[rank : 2 * rank, hid:] = uout[...]
    dinp[0:rank, :] = din[...]
    doutp[0:rank, :] = dout[...]
    acc_a[...] = jnp.zeros_like(acc_a)
    acc_b[...] = jnp.zeros_like(acc_b)
    acc_ad[...] = jnp.zeros_like(acc_ad)
    acc_bd[...] = jnp.zeros_like(acc_bd)

    def to_sib(p, yy):
        return remote(
            part.at[pl.ds(block(p, yy, 1 - c) * rows, rows)],
            sbuf.at[pl.ds((p * 2 + yy) * rows, rows)],
            ss.at[p * 2 + yy], sr.at[p * 2 + yy], SIB,
        )

    def piece_at(p, yy, h):
        return pl.ds((p * 2 + yy) * rows + h * piece, piece)

    def to_side(h):
        return remote(
            sbuf.at[piece_at(z, 1 - y, h)], ybuf.at[pl.ds(h * piece, piece)],
            ys.at[h], yr.at[h], SIDE,
        )

    def along(p, yy, h, kind):
        lead = 0 if kind == UP else 1
        return remote(
            sbuf.at[piece_at(p, yy, h)], zbuf.at[lead, piece_at(p, yy, h)],
            zs.at[p * 2 + yy, h], zr.at[lead, p * 2 + yy, h], kind,
        )

    def wait_sums(p):
        to_sib(p, 0).wait_recv()
        to_sib(p, 1).wait_recv()

    def chip_sum(p, yy, h):
        here = pl.ds(block(p, yy, c) * rows + h * piece, piece)
        total_s[...] = part[here, :].astype(F32) + sbuf[piece_at(p, yy, h), :].astype(F32)

    def add_from(p, yy, h, kind):
        along(p, yy, h, kind).wait_recv()
        total_s[...] += zbuf[0 if kind == UP else 1, piece_at(p, yy, h), :].astype(F32)

    def pass_on(p, h):
        for yy in (0, 1):
            chip_sum(p, yy, h)
            pl.when(jnp.logical_and(p > z, z > 0))(lambda: add_from(p, yy, h, UP))
            pl.when(jnp.logical_and(p < z, z < 3))(lambda: add_from(p, yy, h, DOWN))
            sbuf[piece_at(p, yy, h), :] = total_s[...].astype(BF16)
            pl.when(p > z)(lambda: along(p, yy, h, UP).start())
            pl.when(p < z)(lambda: along(p, yy, h, DOWN).start())

    def pass_all(p):
        wait_sums(p)

        def step(h, _):
            pass_on(p, h)
            return 0

        lax.fori_loop(0, PIECES, step, 0)

    chunk = 64
    expert_lane = lax.broadcasted_iota(jnp.int32, (chunk, LANES), 1)

    def forward(p):
        at = pl.ds(p * plane_rows, plane_rows)
        x = xbuf[at, :]
        low = mm_t(x, ain[...]).astype(BF16)
        low_s[...] = low
        gate_s[...] = mm(x, wg[...]) + ADAPTER_SCALING * mm(low, aout[:, 0:hid])
        up_s[...] = mm(x, wu[...]) + ADAPTER_SCALING * mm(low, aout[:, hid:])

        def step(r, _):
            rr = pl.ds(r * chunk, chunk)
            gate = gate_s[rr, :]
            act = gate * jax.nn.sigmoid(gate)
            hid_s[rr, :] = (act * up_s[rr, :]).astype(BF16)
            return 0

        lax.fori_loop(0, plane_rows // chunk, step, 0)
        hlow_s[...] = mm_t(hid_s[...], dinp[...])

    def backward(p):
        at = pl.ds(p * plane_rows, plane_rows)
        g = gbuf[at, 0:feat]
        glow = mm_t(g, doutp[...])
        gh_s[...] = mm_t(g, wd[...]) + ADAPTER_SCALING * mm(glow.astype(BF16), dinp[...])

        def step(r, _):
            rr = pl.ds(r * chunk, chunk)
            full = pl.ds(p * plane_rows + r * chunk, chunk)
            gh = gh_s[rr, :]
            gate = gate_s[rr, :]
            up = up_s[rr, :]
            sig = jax.nn.sigmoid(gate)
            act = gate * sig
            w = jnp.sum(
                jnp.where(expert_lane == me, gbuf[full, feat:].astype(F32), 0.0), 1, keepdims=True
            )
            wcol_s[rr, :] = jnp.broadcast_to(w, (chunk, LANES))
            dots = jnp.sum(hid_s[rr, :].astype(F32) * gh, 1, keepdims=True)
            high = dots.astype(BF16).astype(F32)
            part[full, feat:] = jnp.where(
                expert_lane == me, high, jnp.where(expert_lane == me + 16, dots - high, 0.0)
            ).astype(BF16)
            gh = gh * w
            gg_s[rr, :] = (gh * up * sig * (1.0 + gate * (1.0 - sig))).astype(BF16)
            gu_s[rr, :] = (gh * act).astype(BF16)
            return 0

        lax.fori_loop(0, plane_rows // chunk, step, 0)
        gg, gu = gg_s[...], gu_s[...]
        lg = (mm_t(gg, aout[:, 0:hid]) + mm_t(gu, aout[:, hid:])).astype(BF16)
        wide_n = min(512, feat)
        for n in range(0, feat, wide_n):
            cols = slice(n, n + wide_n)
            part[at, cols] = (
                mm_t(gg, wg[cols, :])
                + mm_t(gu, wu[cols, :])
                + ADAPTER_SCALING * mm(lg, ain[:, cols])
            ).astype(BF16)
        return glow, lg

    def outer(p, glow, lg):
        at = pl.ds(p * plane_rows, plane_rows)
        w = wcol_s[...]
        acc_a[...] += mm(turned(lg)[0 : 2 * rank], xbuf[at, :])
        low_t = turned(low_s[...])[0 : 2 * rank]
        acc_b[:, 0:hid] += mm(low_t, gg_s[...])
        acc_b[:, hid:] += mm(low_t, gu_s[...])
        acc_ad[...] += mm(turned(w * glow)[0:rank], hid_s[...])
        hlow = hlow_s[...].astype(BF16).astype(F32)
        acc_bd[...] += mm(turned(w * hlow)[0:rank], gbuf[at, 0:feat])

    def body(s, _):
        p = plane_at(s)
        before = plane_at(jnp.maximum(s - 1, 0))
        relays(arrays[0], s)
        wait_sib(arrays[0], p)
        forward(p)
        pl.when(jnp.logical_and(inner == 0, s >= 2))(lambda: pass_all(before))
        relays(arrays[1], s)
        wait_sib(arrays[1], p)
        glow, lg = backward(p)
        to_sib(p, 0).start()
        to_sib(p, 1).start()
        outer(p, glow, lg)
        pl.when(jnp.logical_and(inner == 1, s == 3))(lambda: pass_all(before))
        return 0

    for fetch in fetches:
        fetch.wait()
    lax.fori_loop(0, 4, body, 0)
    last = plane_at(3)
    wait_sums(last)
    pl.when(inner == 1)(lambda: wait_sums(plane_at(1)))

    def tail(h, _):
        pass_on(last, h)
        pl.when(inner == 1)(lambda: pass_on(plane_at(1), h))
        return 0

    lax.fori_loop(0, PIECES, tail, 0)

    ag_out[...] = acc_a[0:rank, :]
    au_out[...] = acc_a[rank : 2 * rank, :]
    bg_out[...] = acc_b[0:rank, 0:hid]
    bu_out[...] = acc_b[rank : 2 * rank, hid:]
    ad_out[...] = acc_ad[...]
    bd_out[...] = acc_bd[...]

    wait_sums(z)

    def arrived(yy, h):
        chip_sum(z, yy, h)
        pl.when(z > 0)(lambda: add_from(z, yy, h, UP))
        pl.when(z < 3)(lambda: add_from(z, yy, h, DOWN))

    def cross(h, _):
        arrived(1 - y, h)
        sbuf[piece_at(z, 1 - y, h), :] = total_s[...].astype(BF16)
        to_side(h).start()
        return 0

    def finish(h, _):
        arrived(y, h)
        to_side(h).wait_recv()
        at = pl.ds(h * piece, piece)
        ybuf[at, :] = (total_s[...] + ybuf[at, :].astype(F32)).astype(BF16)
        return 0

    lax.fori_loop(0, PIECES, cross, 0)
    lax.fori_loop(0, PIECES, finish, 0)
    at = pl.ds(0, rows)
    tok_out[...] = ybuf[at, 0:feat]
    dots = ybuf[at, feat:].astype(F32)
    place = lax.broadcasted_iota(jnp.int32, route.shape, 1)
    result = jnp.zeros(route.shape, F32)
    for k in range(route.shape[1]):
        pick = jnp.logical_or(lane == route[:, k : k + 1], lane == route[:, k : k + 1] + 16)
        value = jnp.sum(jnp.where(pick, dots, 0.0), 1, keepdims=True)
        result = jnp.where(place == k, value, result)
    rw_out[...] = result.T

    def sent(copy):
        copy.wait_send()

    for arr in arrays:
        each_own(arr, sent)

        def settle(p, _):
            pl.when(p != z)(lambda: each_column(arr, p, sent))
            sent(wide(*arr, SIB, block(p, 1 - y, c)))
            return 0

        lax.fori_loop(0, 4, settle, 0)

    def settle_sums(p, _):
        sent(to_sib(p, 0))
        sent(to_sib(p, 1))

        def step(h, _):
            for yy in (0, 1):
                pl.when(p > z)(lambda: sent(along(p, yy, h, UP)))
                pl.when(p < z)(lambda: sent(along(p, yy, h, DOWN)))
            return 0

        lax.fori_loop(0, PIECES, step, 0)
        return 0

    def settle_side(h, _):
        sent(to_side(h))
        return 0

    lax.fori_loop(0, PIECES, settle_side, 0)
    lax.fori_loop(0, 4, settle_sums, 0)


def hand_over(*refs):
    for at in range(8):
        value = refs[at][...]
        refs[8 + at][...] = value if at < 2 else ADAPTER_SCALING * value


def kernel_shards(tokens, out_grad, routes, route_weights, *matrices):
    matrices = [matrix[0] for matrix in matrices]
    rows, feat = tokens.shape
    rank, hid = matrices[4].shape
    wide = feat + LANES
    plane = 4 * rows
    shape = jax.ShapeDtypeStruct
    vmem = pltpu.VMEM
    sem = pltpu.SemaphoreType.DMA
    outs = pl.pallas_call(
        routed_kernel,
        out_shape=(
            shape((rows, feat), BF16),
            shape(routes.shape[::-1], F32),
            shape((rank, feat), F32),
            shape((rank, hid), F32),
            shape((rank, feat), F32),
            shape((rank, hid), F32),
            shape((rank, hid), F32),
            shape((rank, feat), F32),
        ),
        in_specs=[pl.BlockSpec(memory_space=pltpu.VMEM)] * 4
        + [pl.BlockSpec(memory_space=pl.ANY)] * 3
        + [pl.BlockSpec(memory_space=pltpu.VMEM)] * 6,
        out_specs=tuple([pl.BlockSpec(memory_space=pltpu.VMEM)] * 8),
        scratch_shapes=[
            vmem((16 * rows, feat), BF16),
            vmem((16 * rows, wide), BF16),
            vmem((16 * rows, wide), BF16),
            vmem((8 * rows, wide), BF16),
            vmem((rows, wide), BF16),
            vmem((2, 8 * rows, wide), BF16),
            vmem((LANES, feat), BF16),
            vmem((LANES, 2 * hid), BF16),
            vmem((LANES, hid), BF16),
            vmem((LANES, feat), BF16),
            vmem((plane, hid), F32),
            vmem((plane, hid), F32),
            vmem((plane, hid), F32),
            vmem((plane, hid), BF16),
            vmem((plane, hid), BF16),
            vmem((plane, hid), BF16),
            vmem((plane, LANES), BF16),
            vmem((plane, LANES), F32),
            vmem((plane, LANES), F32),
            vmem((2 * rank, feat), F32),
            vmem((2 * rank, 2 * hid), F32),
            vmem((rank, hid), F32),
            vmem((rank, feat), F32),
            vmem((rows // PIECES, wide), F32),
            vmem((feat, hid), BF16), vmem((feat, hid), BF16), vmem((hid, feat), BF16),
            sem((3,)),
            sem((4, 16)), sem((16,)), sem((4, 16)), sem((16,)),
            sem((8,)), sem((8,)),
            sem((PIECES,)), sem((PIECES,)),
            sem((8, PIECES)), sem((2, 8, PIECES)),
        ],
        compiler_params=pltpu.CompilerParams(
            collective_id=0, has_side_effects=True, vmem_limit_bytes=60 * 1024 * 1024
        ),
        cost_estimate=pl.CostEstimate(
            flops=12 * 16 * rows * feat * hid, bytes_accessed=6 * feat * hid + 8 * rows * feat,
            transcendentals=16 * rows * hid,
        ),
    )(tokens, out_grad, routes.T, route_weights.T, *matrices)
    outs = pl.pallas_call(
        hand_over,
        out_shape=tuple(shape(out.shape, out.dtype) for out in outs),
        in_specs=[pl.BlockSpec(memory_space=pltpu.VMEM)] * 8,
        out_specs=tuple([pl.BlockSpec(memory_space=pltpu.VMEM)] * 8),
    )(*outs)
    return (outs[0], outs[1].T) + tuple(out[None] for out in outs[2:])


def slot_ranks(id_block, expert_count):
    flat_ids = id_block.reshape(-1)
    one_hot = (flat_ids[:, None] == jnp.arange(expert_count, dtype=jnp.int32)[None, :]).astype(
        jnp.int32
    )
    earlier = jnp.cumsum(one_hot, 0) - one_hot
    return jnp.sum(earlier * one_hot, 1).reshape(id_block.shape)


def low_rank(factor_matrix, multiplier):
    return lax.dot_general(
        factor_matrix, multiplier, (((1,), (1,)), ((), ())), preferred_element_type=jnp.float32
    ).astype(jnp.bfloat16)


def outer_sum(factor_matrix, multiplier):
    return ADAPTER_SCALING * lax.dot_general(
        factor_matrix, multiplier, (((0,), (0,)), ((), ())), preferred_element_type=jnp.float32
    )


def expert_backward(
    input_rows,
    rows_grad,
    rows_weight,
    gate_weight,
    up_weight,
    down_weight,
    gate_adapter_input,
    gate_adapter_output,
    up_adapter_input,
    up_adapter_output,
    down_adapter_input,
    down_adapter_output,
):
    gate_reduced = low_rank(input_rows, gate_adapter_input)
    up_reduced = low_rank(input_rows, up_adapter_input)
    gate_preactivation = jnp.dot(
        input_rows, gate_weight, preferred_element_type=jnp.float32
    ) + ADAPTER_SCALING * jnp.dot(
        gate_reduced, gate_adapter_output, preferred_element_type=jnp.float32
    )
    up_preactivation = jnp.dot(
        input_rows, up_weight, preferred_element_type=jnp.float32
    ) + ADAPTER_SCALING * jnp.dot(up_reduced, up_adapter_output, preferred_element_type=jnp.float32)
    sigmoid_gate = jax.nn.sigmoid(gate_preactivation)
    activated = gate_preactivation * sigmoid_gate
    hidden_state = (activated * up_preactivation).astype(jnp.bfloat16)
    hidden_reduced = low_rank(hidden_state, down_adapter_input)
    expert_result = (
        jnp.dot(hidden_state, down_weight, preferred_element_type=jnp.float32)
        + ADAPTER_SCALING
        * jnp.dot(hidden_reduced, down_adapter_output, preferred_element_type=jnp.float32)
    ).astype(jnp.bfloat16)
    position_gradient = (
        rows_weight.astype(jnp.float32)[:, None] * rows_grad.astype(jnp.float32)
    ).astype(jnp.bfloat16)
    reduced_gradient = low_rank(position_gradient, down_adapter_output)
    hidden_gradient = lax.dot_general(
        position_gradient, down_weight, (((1,), (1,)), ((), ())), preferred_element_type=jnp.float32
    ) + ADAPTER_SCALING * jnp.dot(
        reduced_gradient, down_adapter_input, preferred_element_type=jnp.float32
    )
    grad_gate = (
        hidden_gradient
        * up_preactivation
        * sigmoid_gate
        * (1.0 + gate_preactivation * (1.0 - sigmoid_gate))
    ).astype(jnp.bfloat16)
    grad_up = (hidden_gradient * activated).astype(jnp.bfloat16)
    gate_reduced_gradient = low_rank(grad_gate, gate_adapter_output)
    up_reduced_gradient = low_rank(grad_up, up_adapter_output)
    gradient_rows = lax.dot_general(
        grad_gate, gate_weight, (((1,), (1,)), ((), ())), preferred_element_type=jnp.float32
    )
    gradient_rows = gradient_rows + lax.dot_general(
        grad_up, up_weight, (((1,), (1,)), ((), ())), preferred_element_type=jnp.float32
    )
    gradient_rows = gradient_rows + ADAPTER_SCALING * (
        jnp.dot(gate_reduced_gradient, gate_adapter_input, preferred_element_type=jnp.float32)
        + jnp.dot(up_reduced_gradient, up_adapter_input, preferred_element_type=jnp.float32)
    )
    adapter_grads = (
        outer_sum(gate_reduced_gradient, input_rows),
        outer_sum(gate_reduced, grad_gate),
        outer_sum(up_reduced_gradient, input_rows),
        outer_sum(up_reduced, grad_up),
        outer_sum(reduced_gradient, hidden_state),
        outer_sum(hidden_reduced, position_gradient),
    )
    return (gradient_rows.astype(jnp.bfloat16), expert_result, adapter_grads)


def shards(
    tokens,
    out_grad,
    routes,
    route_weights,
    gate_weight,
    up_weight,
    down_weight,
    gate_adapter_input,
    gate_adapter_output,
    up_adapter_input,
    up_adapter_output,
    down_adapter_input,
    down_adapter_output,
):
    tok_rows, features = tokens.shape
    top_count = routes.shape[1]
    peer_count = lax.axis_size("expert")
    experts = peer_count * gate_weight.shape[0]
    capacity = tok_rows * top_count * 5 // (4 * experts)
    targets = routes * capacity + slot_ranks(routes, experts)
    matches = jnp.arange(experts * capacity, dtype=jnp.int32)[:, None, None] == targets[None, :, :]
    placing = jnp.any(matches, -1).astype(jnp.bfloat16)
    slot_weight = jnp.sum(
        jnp.where(matches, route_weights.astype(jnp.float32)[None, :, :], 0.0), (1, 2)
    ).astype(jnp.bfloat16)
    sent_rows = jnp.dot(placing, tokens, preferred_element_type=jnp.float32).astype(jnp.bfloat16)
    sent_grads = jnp.dot(placing, out_grad, preferred_element_type=jnp.float32).astype(jnp.bfloat16)
    got_rows, got_grads, got_weight = (
        lax.all_to_all(
            sent_rows.reshape(experts, capacity, features),
            "expert",
            split_axis=0,
            concat_axis=0,
            tiled=True,
        ),
        lax.all_to_all(
            sent_grads.reshape(experts, capacity, features),
            "expert",
            split_axis=0,
            concat_axis=0,
            tiled=True,
        ),
        lax.all_to_all(
            slot_weight.reshape(experts, capacity),
            "expert",
            split_axis=0,
            concat_axis=0,
            tiled=True,
        ),
    )
    gradient_rows, expert_result, adapter_grads = expert_backward(
        got_rows.reshape(-1, features),
        got_grads.reshape(-1, features),
        got_weight.reshape(-1),
        gate_weight[0],
        up_weight[0],
        down_weight[0],
        gate_adapter_input[0],
        gate_adapter_output[0],
        up_adapter_input[0],
        up_adapter_output[0],
        down_adapter_input[0],
        down_adapter_output[0],
    )
    dots_here = jnp.sum(
        got_grads.reshape(-1, features).astype(jnp.float32) * expert_result.astype(jnp.float32), -1
    )
    back_rows = lax.all_to_all(
        gradient_rows.reshape(peer_count, capacity, features),
        "expert",
        split_axis=0,
        concat_axis=0,
        tiled=True,
    )
    slot_dots = lax.all_to_all(
        dots_here.reshape(peer_count, capacity), "expert", split_axis=0, concat_axis=0, tiled=True
    ).reshape(-1)
    grad_tokens = lax.dot_general(
        placing,
        back_rows.reshape(-1, features),
        (((0,), (0,)), ((), ())),
        preferred_element_type=jnp.float32,
    ).astype(jnp.bfloat16)
    grad_weights = jnp.take(slot_dots, targets.reshape(-1)).reshape(tok_rows, top_count)
    return (
        grad_tokens,
        grad_weights,
        adapter_grads[0][None],
        adapter_grads[1][None],
        adapter_grads[2][None],
        adapter_grads[3][None],
        adapter_grads[4][None],
        adapter_grads[5][None],
    )


def solution(mesh):
    return jax.shard_map(
        kernel_shards if mesh.shape["expert"] == 16 else shards,
        mesh=mesh,
        in_specs=(
            P(("groups", "expert"), None),
            P(("groups", "expert"), None),
            P(("groups", "expert"), None),
            P(("groups", "expert"), None),
            P("expert", None, None),
            P("expert", None, None),
            P("expert", None, None),
            P("expert", None, None),
            P("expert", None, None),
            P("expert", None, None),
            P("expert", None, None),
            P("expert", None, None),
            P("expert", None, None),
        ),
        out_specs=(
            P(("groups", "expert"), None),
            P(("groups", "expert"), None),
            P(("groups", "expert"), None, None),
            P(("groups", "expert"), None, None),
            P(("groups", "expert"), None, None),
            P(("groups", "expert"), None, None),
            P(("groups", "expert"), None, None),
            P(("groups", "expert"), None, None),
        ),
        check_vma=False,
    )
```

```python
import jax
import jax.numpy as jnp
from jax import lax
from jax.experimental import pallas as pl
from jax.experimental.pallas import tpu as pltpu
from jax.sharding import PartitionSpec as P

ADAPTER_SCALING = 0.5
LANES = 128
PIECES = 4
SIB, SIDE, UP, DOWN = 0, 1, 2, 3
F32, BF16 = jnp.float32, jnp.bfloat16


def mm(a, b):
    return jnp.dot(a, b, preferred_element_type=F32)


def mm_t(a, b):
    return lax.dot_general(a, b, (((1,), (1,)), ((), ())), preferred_element_type=F32)


def turned(value):
    return value.astype(F32).T.astype(BF16)


def routed_kernel(
    x_ref, g_ref, routes_ref, weights_ref, wg_far, wu_far, wd_far, gin, gout, uin, uout, din, dout,
    tok_out, rw_out, ag_out, bg_out, au_out, bu_out, ad_out, bd_out,
    xbuf, gbuf, part, sbuf, ybuf, zbuf,
    ain, aout, dinp, doutp, gate_s, up_s, gh_s, hid_s, gg_s, gu_s, low_s, hlow_s, wcol_s,
    acc_a, acc_b, acc_ad, acc_bd, total_s, wg, wu, wd, wsem,
    xs, xr, gs, gr, ss, sr, ys, yr, zs, zr,
):
    rows, feat = x_ref.shape
    rank, hid = gout.shape
    plane_rows = 4 * rows
    piece = rows // PIECES
    me = lax.axis_index("expert")
    z, y, c = me // 4, (me // 2) % 2, me % 2
    half = z // 2
    inner = (z % 3 + 1) // 2
    target = {SIB: me + 1 - 2 * c, SIDE: me + 2 - 4 * y, UP: (me + 4) % 16, DOWN: (me + 12) % 16}

    def plane_at(s):
        p = s + inner * (1 - s // 2) * (1 - 2 * s)
        return p + half * (3 - 2 * p)

    def block(p, yy, cc):
        return p * 4 + yy * 2 + cc

    def remote(src, dst, send, recv, kind):
        return pltpu.make_async_remote_copy(
            src_ref=src, dst_ref=dst, send_sem=send, recv_sem=recv,
            device_id={"expert": target[kind]}, device_id_type=pl.DeviceIdType.MESH,
        )

    barrier = pltpu.get_barrier_semaphore()

    def greet(kind):
        pl.semaphore_signal(
            barrier, inc=1, device_id={"expert": target[kind]},
            device_id_type=pl.DeviceIdType.MESH,
        )

    greet(SIB)
    greet(SIDE)
    pl.when(z < 3)(lambda: greet(UP))
    pl.when(z > 0)(lambda: greet(DOWN))

    own = pl.ds(me * rows, rows)
    xbuf[own, :] = x_ref[...]
    gbuf[own, 0:feat] = g_ref[...]
    lane = lax.broadcasted_iota(jnp.int32, (rows, LANES), 1)
    route = routes_ref[...].astype(F32).T.astype(jnp.int32)
    route_w = weights_ref[...].astype(F32).T
    table = jnp.zeros((rows, LANES), F32)
    for k in range(route.shape[1]):
        table = jnp.where(lane == route[:, k : k + 1], route_w[:, k : k + 1], table)
    gbuf[own, feat:] = table.astype(BF16)

    pl.semaphore_wait(barrier, 3 + inner)

    def wide(buf, send, recv, kind, b):
        at = buf.at[pl.ds(b * rows, rows)]
        return remote(at, at, send.at[kind, b], recv.at[b], kind)

    arrays = ((xbuf, xs, xr), (gbuf, gs, gr))

    def each_own(arr, act):
        act(wide(*arr, SIDE, me))
        pl.when(z < 3)(lambda: act(wide(*arr, UP, me)))
        pl.when(z > 0)(lambda: act(wide(*arr, DOWN, me)))
        act(wide(*arr, SIB, me))

    def each_column(arr, p, act):
        b = block(p, y, c)
        pl.when(jnp.logical_and(p < z, z < 3))(lambda: act(wide(*arr, UP, b)))
        pl.when(jnp.logical_and(p > z, z > 0))(lambda: act(wide(*arr, DOWN, b)))
        act(wide(*arr, SIDE, b))
        act(wide(*arr, SIB, b))

    def start(copy):
        copy.start()

    def relay_z(arr, p):
        wide(*arr, SIB, block(p, y, c)).wait_recv()
        each_column(arr, p, start)

    def relay_y(arr, p):
        b = block(p, 1 - y, c)
        wide(*arr, SIB, b).wait_recv()
        wide(*arr, SIB, b).start()

    def wait_sib(arr, p):
        wide(*arr, SIB, block(p, 0, 1 - c)).wait_recv()
        wide(*arr, SIB, block(p, 1, 1 - c)).wait_recv()

    def relays(arr, s):
        relay_y(arr, plane_at(s))

        @pl.when(s < 3 - inner)
        def _():
            relay_z(arr, plane_at(s + 1 + inner * s))

        @pl.when(jnp.logical_and(inner == 1, s == 0))
        def _():
            relay_z(arr, plane_at(2))

    for arr in arrays:
        each_own(arr, start)

    fetches = [
        pltpu.make_async_copy(far, near, wsem.at[at])
        for at, (far, near) in enumerate(((wg_far, wg), (wu_far, wu), (wd_far, wd)))
    ]
    for fetch in fetches:
        fetch.start()

    ain[...] = jnp.zeros_like(ain)
    aout[...] = jnp.zeros_like(aout)
    dinp[...] = jnp.zeros_like(dinp)
    doutp[...] = jnp.zeros_like(doutp)
    ain[0:rank, :] = gin[...]
    ain[rank : 2 * rank, :] = uin[...]
    aout[0:rank, 0:hid] = gout[...]
    aout[rank : 2 * rank, hid:] = uout[...]
    dinp[0:rank, :] = din[...]
    doutp[0:rank, :] = dout[...]
    acc_a[...] = jnp.zeros_like(acc_a)
    acc_b[...] = jnp.zeros_like(acc_b)
    acc_ad[...] = jnp.zeros_like(acc_ad)
    acc_bd[...] = jnp.zeros_like(acc_bd)

    def to_sib(p, yy):
        return remote(
            part.at[pl.ds(block(p, yy, 1 - c) * rows, rows)],
            sbuf.at[pl.ds((p * 2 + yy) * rows, rows)],
            ss.at[p * 2 + yy], sr.at[p * 2 + yy], SIB,
        )

    def piece_at(p, yy, h):
        return pl.ds((p * 2 + yy) * rows + h * piece, piece)

    def to_side(p, h):
        return remote(
            sbuf.at[piece_at(p, 1 - y, h)], ybuf.at[pl.ds(p * rows + h * piece, piece)],
            ys.at[p, h], yr.at[p, h], SIDE,
        )

    def cross_first(p, h):
        chip_sum(p, 1 - y, h)
        sbuf[piece_at(p, 1 - y, h), :] = total_s[...].astype(BF16)
        to_side(p, h).start()

    def crossed(p, h):
        to_side(p, h).wait_recv()
        total_s[...] += ybuf[pl.ds(p * rows + h * piece, piece), :].astype(F32)

    def pass_end(p, h):
        chip_sum(p, y, h)
        crossed(p, h)
        pl.when(jnp.logical_and(p == 3, z > 0))(lambda: add_from(p, y, h, UP))
        pl.when(jnp.logical_and(p == 0, z < 3))(lambda: add_from(p, y, h, DOWN))
        sbuf[piece_at(p, y, h), :] = total_s[...].astype(BF16)
        pl.when(p == 3)(lambda: along(p, y, h, UP).start())
        pl.when(p == 0)(lambda: along(p, y, h, DOWN).start())

    def along(p, yy, h, kind):
        lead = 0 if kind == UP else 1
        return remote(
            sbuf.at[piece_at(p, yy, h)], zbuf.at[lead, piece_at(p, yy, h)],
            zs.at[p * 2 + yy, h], zr.at[lead, p * 2 + yy, h], kind,
        )

    def wait_sums(p):
        to_sib(p, 0).wait_recv()
        to_sib(p, 1).wait_recv()

    def chip_sum(p, yy, h):
        here = pl.ds(block(p, yy, c) * rows + h * piece, piece)
        total_s[...] = part[here, :].astype(F32) + sbuf[piece_at(p, yy, h), :].astype(F32)

    def add_from(p, yy, h, kind):
        along(p, yy, h, kind).wait_recv()
        total_s[...] += zbuf[0 if kind == UP else 1, piece_at(p, yy, h), :].astype(F32)

    def pass_on(p, h):
        for yy in (0, 1):
            chip_sum(p, yy, h)
            pl.when(jnp.logical_and(p > z, z > 0))(lambda: add_from(p, yy, h, UP))
            pl.when(jnp.logical_and(p < z, z < 3))(lambda: add_from(p, yy, h, DOWN))
            sbuf[piece_at(p, yy, h), :] = total_s[...].astype(BF16)
            pl.when(p > z)(lambda: along(p, yy, h, UP).start())
            pl.when(p < z)(lambda: along(p, yy, h, DOWN).start())

    def pass_all(p):
        wait_sums(p)

        def step(h, _):
            pass_on(p, h)
            return 0

        lax.fori_loop(0, PIECES, step, 0)

    chunk = 64
    expert_lane = lax.broadcasted_iota(jnp.int32, (chunk, LANES), 1)

    def forward(p):
        at = pl.ds(p * plane_rows, plane_rows)
        x = xbuf[at, :]
        low = mm_t(x, ain[...]).astype(BF16)
        low_s[...] = low
        gate_s[...] = mm(x, wg[...]) + ADAPTER_SCALING * mm(low, aout[:, 0:hid])
        up_s[...] = mm(x, wu[...]) + ADAPTER_SCALING * mm(low, aout[:, hid:])

        def step(r, _):
            rr = pl.ds(r * chunk, chunk)
            gate = gate_s[rr, :]
            act = gate * jax.nn.sigmoid(gate)
            hid_s[rr, :] = (act * up_s[rr, :]).astype(BF16)
            return 0

        lax.fori_loop(0, plane_rows // chunk, step, 0)
        hlow_s[...] = mm_t(hid_s[...], dinp[...])

    def backward(p):
        at = pl.ds(p * plane_rows, plane_rows)
        g = gbuf[at, 0:feat]
        glow = mm_t(g, doutp[...])
        gh_s[...] = mm_t(g, wd[...]) + ADAPTER_SCALING * mm(glow.astype(BF16), dinp[...])

        def step(r, _):
            rr = pl.ds(r * chunk, chunk)
            full = pl.ds(p * plane_rows + r * chunk, chunk)
            gh = gh_s[rr, :]
            gate = gate_s[rr, :]
            up = up_s[rr, :]
            sig = jax.nn.sigmoid(gate)
            act = gate * sig
            w = jnp.sum(
                jnp.where(expert_lane == me, gbuf[full, feat:].astype(F32), 0.0), 1, keepdims=True
            )
            wcol_s[rr, :] = jnp.broadcast_to(w, (chunk, LANES))
            dots = jnp.sum(hid_s[rr, :].astype(F32) * gh, 1, keepdims=True)
            high = dots.astype(BF16).astype(F32)
            part[full, feat:] = jnp.where(
                expert_lane == me, high, jnp.where(expert_lane == me + 16, dots - high, 0.0)
            ).astype(BF16)
            gh = gh * w
            gg_s[rr, :] = (gh * up * sig * (1.0 + gate * (1.0 - sig))).astype(BF16)
            gu_s[rr, :] = (gh * act).astype(BF16)
            return 0

        lax.fori_loop(0, plane_rows // chunk, step, 0)
        gg, gu = gg_s[...], gu_s[...]
        lg = (mm_t(gg, aout[:, 0:hid]) + mm_t(gu, aout[:, hid:])).astype(BF16)
        wide_n = min(512, feat)
        for n in range(0, feat, wide_n):
            cols = slice(n, n + wide_n)
            part[at, cols] = (
                mm_t(gg, wg[cols, :])
                + mm_t(gu, wu[cols, :])
                + ADAPTER_SCALING * mm(lg, ain[:, cols])
            ).astype(BF16)
        return glow, lg

    def outer(p, glow, lg):
        at = pl.ds(p * plane_rows, plane_rows)
        w = wcol_s[...]
        acc_a[...] += mm(turned(lg)[0 : 2 * rank], xbuf[at, :])
        low_t = turned(low_s[...])[0 : 2 * rank]
        acc_b[:, 0:hid] += mm(low_t, gg_s[...])
        acc_b[:, hid:] += mm(low_t, gu_s[...])
        acc_ad[...] += mm(turned(w * glow)[0:rank], hid_s[...])
        hlow = hlow_s[...].astype(BF16).astype(F32)
        acc_bd[...] += mm(turned(w * hlow)[0:rank], gbuf[at, 0:feat])

    def body(s, _):
        p = plane_at(s)
        before = plane_at(jnp.maximum(s - 1, 0))
        relays(arrays[0], s)
        wait_sib(arrays[0], p)
        forward(p)
        pl.when(jnp.logical_and(inner == 0, s >= 2))(lambda: pass_all(before))
        relays(arrays[1], s)
        wait_sib(arrays[1], p)
        glow, lg = backward(p)
        to_sib(p, 0).start()
        to_sib(p, 1).start()
        outer(p, glow, lg)
        pl.when(jnp.logical_and(inner == 1, s == 3))(lambda: pass_all(before))
        return 0

    for fetch in fetches:
        fetch.wait()
    lax.fori_loop(0, 4, body, 0)
    last = plane_at(3)
    wait_sums(last)
    pl.when(inner == 1)(lambda: wait_sums(plane_at(1)))

    def tail_cross(h, _):
        cross_first(last, h)
        return 0

    def tail_cross_near(h, _):
        cross_first(plane_at(1), h)
        return 0

    def tail(h, _):
        pass_end(last, h)
        pl.when(inner == 1)(lambda: pass_end(plane_at(1), h))
        return 0

    lax.fori_loop(0, PIECES, tail_cross, 0)

    @pl.when(inner == 1)
    def _():
        lax.fori_loop(0, PIECES, tail_cross_near, 0)

    wait_sums(z)

    @pl.when(inner == 0)
    def _():
        def own_cross(h, _):
            cross_first(z, h)
            return 0

        lax.fori_loop(0, PIECES, own_cross, 0)

    lax.fori_loop(0, PIECES, tail, 0)

    ag_out[...] = acc_a[0:rank, :]
    au_out[...] = acc_a[rank : 2 * rank, :]
    bg_out[...] = acc_b[0:rank, 0:hid]
    bu_out[...] = acc_b[rank : 2 * rank, hid:]
    ad_out[...] = acc_ad[...]
    bd_out[...] = acc_bd[...]

    def arrived(yy, h):
        chip_sum(z, yy, h)
        pl.when(z > 0)(lambda: add_from(z, yy, h, UP))
        pl.when(z < 3)(lambda: add_from(z, yy, h, DOWN))

    def cross(h, _):
        arrived(1 - y, h)
        sbuf[piece_at(z, 1 - y, h), :] = total_s[...].astype(BF16)
        to_side(z, h).start()
        return 0

    def finish(h, _):
        arrived(y, h)
        crossed(z, h)
        ybuf[pl.ds(z * rows + h * piece, piece), :] = total_s[...].astype(BF16)
        return 0

    @pl.when(inner == 1)
    def _():
        lax.fori_loop(0, PIECES, cross, 0)

    lax.fori_loop(0, PIECES, finish, 0)
    at = pl.ds(z * rows, rows)
    tok_out[...] = ybuf[at, 0:feat]
    dots = ybuf[at, feat:].astype(F32)
    place = lax.broadcasted_iota(jnp.int32, route.shape, 1)
    result = jnp.zeros(route.shape, F32)
    for k in range(route.shape[1]):
        pick = jnp.logical_or(lane == route[:, k : k + 1], lane == route[:, k : k + 1] + 16)
        value = jnp.sum(jnp.where(pick, dots, 0.0), 1, keepdims=True)
        result = jnp.where(place == k, value, result)
    rw_out[...] = result.T

    def sent(copy):
        copy.wait_send()

    for arr in arrays:
        each_own(arr, sent)

        def settle(p, _):
            pl.when(p != z)(lambda: each_column(arr, p, sent))
            sent(wide(*arr, SIB, block(p, 1 - y, c)))
            return 0

        lax.fori_loop(0, 4, settle, 0)

    def settle_sums(p, _):
        sent(to_sib(p, 0))
        sent(to_sib(p, 1))

        end = 1 - (p % 3 + 1) // 2

        def step(h, _):
            for yy in (0, 1):
                used = jnp.logical_or(end == 0, yy == y)
                pl.when(jnp.logical_and(used, p > z))(lambda: sent(along(p, yy, h, UP)))
                pl.when(jnp.logical_and(used, p < z))(lambda: sent(along(p, yy, h, DOWN)))
            pl.when(jnp.logical_or(end == 1, p == z))(lambda: sent(to_side(p, h)))
            return 0

        lax.fori_loop(0, PIECES, step, 0)
        return 0

    lax.fori_loop(0, 4, settle_sums, 0)


def hand_over(*refs):
    for at in range(8):
        value = refs[at][...]
        refs[8 + at][...] = value if at < 2 else ADAPTER_SCALING * value


def kernel_shards(tokens, out_grad, routes, route_weights, *matrices):
    matrices = [matrix[0] for matrix in matrices]
    rows, feat = tokens.shape
    rank, hid = matrices[4].shape
    wide = feat + LANES
    plane = 4 * rows
    shape = jax.ShapeDtypeStruct
    vmem = pltpu.VMEM
    sem = pltpu.SemaphoreType.DMA
    outs = pl.pallas_call(
        routed_kernel,
        out_shape=(
            shape((rows, feat), BF16),
            shape(routes.shape[::-1], F32),
            shape((rank, feat), F32),
            shape((rank, hid), F32),
            shape((rank, feat), F32),
            shape((rank, hid), F32),
            shape((rank, hid), F32),
            shape((rank, feat), F32),
        ),
        in_specs=[pl.BlockSpec(memory_space=pltpu.VMEM)] * 4
        + [pl.BlockSpec(memory_space=pl.ANY)] * 3
        + [pl.BlockSpec(memory_space=pltpu.VMEM)] * 6,
        out_specs=tuple([pl.BlockSpec(memory_space=pltpu.VMEM)] * 8),
        scratch_shapes=[
            vmem((16 * rows, feat), BF16),
            vmem((16 * rows, wide), BF16),
            vmem((16 * rows, wide), BF16),
            vmem((8 * rows, wide), BF16),
            vmem((4 * rows, wide), BF16),
            vmem((2, 8 * rows, wide), BF16),
            vmem((LANES, feat), BF16),
            vmem((LANES, 2 * hid), BF16),
            vmem((LANES, hid), BF16),
            vmem((LANES, feat), BF16),
            vmem((plane, hid), F32),
            vmem((plane, hid), F32),
            vmem((plane, hid), F32),
            vmem((plane, hid), BF16),
            vmem((plane, hid), BF16),
            vmem((plane, hid), BF16),
            vmem((plane, LANES), BF16),
            vmem((plane, LANES), F32),
            vmem((plane, LANES), F32),
            vmem((2 * rank, feat), F32),
            vmem((2 * rank, 2 * hid), F32),
            vmem((rank, hid), F32),
            vmem((rank, feat), F32),
            vmem((rows // PIECES, wide), F32),
            vmem((feat, hid), BF16), vmem((feat, hid), BF16), vmem((hid, feat), BF16),
            sem((3,)),
            sem((4, 16)), sem((16,)), sem((4, 16)), sem((16,)),
            sem((8,)), sem((8,)),
            sem((4, PIECES)), sem((4, PIECES)),
            sem((8, PIECES)), sem((2, 8, PIECES)),
        ],
        compiler_params=pltpu.CompilerParams(
            collective_id=0, has_side_effects=True, vmem_limit_bytes=60 * 1024 * 1024
        ),
        cost_estimate=pl.CostEstimate(
            flops=12 * 16 * rows * feat * hid, bytes_accessed=6 * feat * hid + 8 * rows * feat,
            transcendentals=16 * rows * hid,
        ),
    )(tokens, out_grad, routes.T, route_weights.T, *matrices)
    outs = pl.pallas_call(
        hand_over,
        out_shape=tuple(shape(out.shape, out.dtype) for out in outs),
        in_specs=[pl.BlockSpec(memory_space=pltpu.VMEM)] * 8,
        out_specs=tuple([pl.BlockSpec(memory_space=pltpu.VMEM)] * 8),
    )(*outs)
    return (outs[0], outs[1].T) + tuple(out[None] for out in outs[2:])


def slot_ranks(id_block, expert_count):
    flat_ids = id_block.reshape(-1)
    one_hot = (flat_ids[:, None] == jnp.arange(expert_count, dtype=jnp.int32)[None, :]).astype(
        jnp.int32
    )
    earlier = jnp.cumsum(one_hot, 0) - one_hot
    return jnp.sum(earlier * one_hot, 1).reshape(id_block.shape)


def low_rank(factor_matrix, multiplier):
    return lax.dot_general(
        factor_matrix, multiplier, (((1,), (1,)), ((), ())), preferred_element_type=jnp.float32
    ).astype(jnp.bfloat16)


def outer_sum(factor_matrix, multiplier):
    return ADAPTER_SCALING * lax.dot_general(
        factor_matrix, multiplier, (((0,), (0,)), ((), ())), preferred_element_type=jnp.float32
    )


def expert_backward(
    input_rows,
    rows_grad,
    rows_weight,
    gate_weight,
    up_weight,
    down_weight,
    gate_adapter_input,
    gate_adapter_output,
    up_adapter_input,
    up_adapter_output,
    down_adapter_input,
    down_adapter_output,
):
    gate_reduced = low_rank(input_rows, gate_adapter_input)
    up_reduced = low_rank(input_rows, up_adapter_input)
    gate_preactivation = jnp.dot(
        input_rows, gate_weight, preferred_element_type=jnp.float32
    ) + ADAPTER_SCALING * jnp.dot(
        gate_reduced, gate_adapter_output, preferred_element_type=jnp.float32
    )
    up_preactivation = jnp.dot(
        input_rows, up_weight, preferred_element_type=jnp.float32
    ) + ADAPTER_SCALING * jnp.dot(up_reduced, up_adapter_output, preferred_element_type=jnp.float32)
    sigmoid_gate = jax.nn.sigmoid(gate_preactivation)
    activated = gate_preactivation * sigmoid_gate
    hidden_state = (activated * up_preactivation).astype(jnp.bfloat16)
    hidden_reduced = low_rank(hidden_state, down_adapter_input)
    expert_result = (
        jnp.dot(hidden_state, down_weight, preferred_element_type=jnp.float32)
        + ADAPTER_SCALING
        * jnp.dot(hidden_reduced, down_adapter_output, preferred_element_type=jnp.float32)
    ).astype(jnp.bfloat16)
    position_gradient = (
        rows_weight.astype(jnp.float32)[:, None] * rows_grad.astype(jnp.float32)
    ).astype(jnp.bfloat16)
    reduced_gradient = low_rank(position_gradient, down_adapter_output)
    hidden_gradient = lax.dot_general(
        position_gradient, down_weight, (((1,), (1,)), ((), ())), preferred_element_type=jnp.float32
    ) + ADAPTER_SCALING * jnp.dot(
        reduced_gradient, down_adapter_input, preferred_element_type=jnp.float32
    )
    grad_gate = (
        hidden_gradient
        * up_preactivation
        * sigmoid_gate
        * (1.0 + gate_preactivation * (1.0 - sigmoid_gate))
    ).astype(jnp.bfloat16)
    grad_up = (hidden_gradient * activated).astype(jnp.bfloat16)
    gate_reduced_gradient = low_rank(grad_gate, gate_adapter_output)
    up_reduced_gradient = low_rank(grad_up, up_adapter_output)
    gradient_rows = lax.dot_general(
        grad_gate, gate_weight, (((1,), (1,)), ((), ())), preferred_element_type=jnp.float32
    )
    gradient_rows = gradient_rows + lax.dot_general(
        grad_up, up_weight, (((1,), (1,)), ((), ())), preferred_element_type=jnp.float32
    )
    gradient_rows = gradient_rows + ADAPTER_SCALING * (
        jnp.dot(gate_reduced_gradient, gate_adapter_input, preferred_element_type=jnp.float32)
        + jnp.dot(up_reduced_gradient, up_adapter_input, preferred_element_type=jnp.float32)
    )
    adapter_grads = (
        outer_sum(gate_reduced_gradient, input_rows),
        outer_sum(gate_reduced, grad_gate),
        outer_sum(up_reduced_gradient, input_rows),
        outer_sum(up_reduced, grad_up),
        outer_sum(reduced_gradient, hidden_state),
        outer_sum(hidden_reduced, position_gradient),
    )
    return (gradient_rows.astype(jnp.bfloat16), expert_result, adapter_grads)


def shards(
    tokens,
    out_grad,
    routes,
    route_weights,
    gate_weight,
    up_weight,
    down_weight,
    gate_adapter_input,
    gate_adapter_output,
    up_adapter_input,
    up_adapter_output,
    down_adapter_input,
    down_adapter_output,
):
    tok_rows, features = tokens.shape
    top_count = routes.shape[1]
    peer_count = lax.axis_size("expert")
    experts = peer_count * gate_weight.shape[0]
    capacity = tok_rows * top_count * 5 // (4 * experts)
    targets = routes * capacity + slot_ranks(routes, experts)
    matches = jnp.arange(experts * capacity, dtype=jnp.int32)[:, None, None] == targets[None, :, :]
    placing = jnp.any(matches, -1).astype(jnp.bfloat16)
    slot_weight = jnp.sum(
        jnp.where(matches, route_weights.astype(jnp.float32)[None, :, :], 0.0), (1, 2)
    ).astype(jnp.bfloat16)
    sent_rows = jnp.dot(placing, tokens, preferred_element_type=jnp.float32).astype(jnp.bfloat16)
    sent_grads = jnp.dot(placing, out_grad, preferred_element_type=jnp.float32).astype(jnp.bfloat16)
    got_rows, got_grads, got_weight = (
        lax.all_to_all(
            sent_rows.reshape(experts, capacity, features),
            "expert",
            split_axis=0,
            concat_axis=0,
            tiled=True,
        ),
        lax.all_to_all(
            sent_grads.reshape(experts, capacity, features),
            "expert",
            split_axis=0,
            concat_axis=0,
            tiled=True,
        ),
        lax.all_to_all(
            slot_weight.reshape(experts, capacity),
            "expert",
            split_axis=0,
            concat_axis=0,
            tiled=True,
        ),
    )
    gradient_rows, expert_result, adapter_grads = expert_backward(
        got_rows.reshape(-1, features),
        got_grads.reshape(-1, features),
        got_weight.reshape(-1),
        gate_weight[0],
        up_weight[0],
        down_weight[0],
        gate_adapter_input[0],
        gate_adapter_output[0],
        up_adapter_input[0],
        up_adapter_output[0],
        down_adapter_input[0],
        down_adapter_output[0],
    )
    dots_here = jnp.sum(
        got_grads.reshape(-1, features).astype(jnp.float32) * expert_result.astype(jnp.float32), -1
    )
    back_rows = lax.all_to_all(
        gradient_rows.reshape(peer_count, capacity, features),
        "expert",
        split_axis=0,
        concat_axis=0,
        tiled=True,
    )
    slot_dots = lax.all_to_all(
        dots_here.reshape(peer_count, capacity), "expert", split_axis=0, concat_axis=0, tiled=True
    ).reshape(-1)
    grad_tokens = lax.dot_general(
        placing,
        back_rows.reshape(-1, features),
        (((0,), (0,)), ((), ())),
        preferred_element_type=jnp.float32,
    ).astype(jnp.bfloat16)
    grad_weights = jnp.take(slot_dots, targets.reshape(-1)).reshape(tok_rows, top_count)
    return (
        grad_tokens,
        grad_weights,
        adapter_grads[0][None],
        adapter_grads[1][None],
        adapter_grads[2][None],
        adapter_grads[3][None],
        adapter_grads[4][None],
        adapter_grads[5][None],
    )


def solution(mesh):
    return jax.shard_map(
        kernel_shards if mesh.shape["expert"] == 16 else shards,
        mesh=mesh,
        in_specs=(
            P(("groups", "expert"), None),
            P(("groups", "expert"), None),
            P(("groups", "expert"), None),
            P(("groups", "expert"), None),
            P("expert", None, None),
            P("expert", None, None),
            P("expert", None, None),
            P("expert", None, None),
            P("expert", None, None),
            P("expert", None, None),
            P("expert", None, None),
            P("expert", None, None),
            P("expert", None, None),
        ),
        out_specs=(
            P(("groups", "expert"), None),
            P(("groups", "expert"), None),
            P(("groups", "expert"), None, None),
            P(("groups", "expert"), None, None),
            P(("groups", "expert"), None, None),
            P(("groups", "expert"), None, None),
            P(("groups", "expert"), None, None),
            P(("groups", "expert"), None, None),
        ),
        check_vma=False,
    )
```
